32 devices in a mesh: groups: 2 (over y), section: 2 (over core), ep: 4 (over z), tp: 2 (over x).
Axes of the slice: x: 2, y: 2, z: 4, core: 2. Of those that a mesh axis runs over, the one named last changes fastest.
Arguments:
- tokens: bfloat16 [16384, 6144], P(('groups', 'section', 'ep'), 'tp'), parts along dimension 0, may hold values from -6 to 6
- w_kv: bfloat16 [6144, 2048], P(('section', 'ep'), 'tp'), may hold values from -0.078125 to 0.078125
- page_target: int32 [1024, 1], P(('groups', 'section', 'ep')), parts along dimension 0, may hold values from 0 to 7; in each aligned block of 64 rows (0 to 63, 64 to 127, ...) at most 16 rows name the same one
- queries: bfloat16 [256, 2, 6144], P(('groups', 'section', 'ep'), None, 'tp'), parts along dimension 0, may hold values from -110 to 110
- decoded_keys: bfloat16 [256, 2, 1024], P(('groups', 'section', 'ep'), None, 'tp'), parts along dimension 0, may hold values from -4 to 4
- decoded_values: bfloat16 [256, 2, 1024], P(('groups', 'section', 'ep'), None, 'tp'), parts along dimension 0, may hold values from -6 to 6
Outputs:
- attended: bfloat16 [256, 2, 6144], P(('groups', 'section', 'ep'), None, 'tp'), parts along dimension 0
The draws below stay inside these ranges and needn't reach their ends.
There are 2 independent parts, one for each index of `groups`. The reference program is written for one: setup_inputs(seed, part) draws one part's arguments, and reference() takes and returns one part's arrays. A program takes and returns all parts, laid end to end along the dimension named above; an argument that names none is the same for every part. Nothing has to cross between parts.
Inputs may be any that keep to these rules, and one draw needn't show every extreme that they name: `page_target`: every request owns at least one page; request r is decoded by the forks 16 * r to 16 * r + 15; among the 64 pages of one device at most 16 belong to one request, and in every draw some device holds exactly 16 pages of one request.
All inputs are finite; a program needn't handle non-finite values.
Results may differ from the reference program's by a relative error of at most 0.0077.
Values may be sent and summed in bfloat16 or wider, within the bound.
A program may use at most 128 MiB of HBM per device.

```python
import math
import jax
import jax.numpy as jnp
import numpy as np
from jax import lax

D = 6144
QUERY_HEADS = 48
KEY_VALUE_HEADS = 8
HEAD_SIZE = 128
PAGE = 16
PG_DEV = 64
REQUEST_FORKS = 16
FORK_STEPS = 2
PAGES = 512
PROMPT_TOKENS = 8192
TOTAL_FORKS = 128
CAP = 16
KV_COLS = 2048
N_SECTION = 2
N_EP = 4


def shared_keys(key, align_share):
    total_rows = REQUEST_FORKS * N_SECTION * N_EP
    base_sample = jnp.clip(jax.random.normal(jax.random.fold_in(key, 11), (total_rows, FORK_STEPS, KEY_VALUE_HEADS * HEAD_SIZE), jnp.float32), -4.0, 4.0)
    aligned = jax.random.uniform(jax.random.fold_in(key, 12), (total_rows,), jnp.float32) < align_share
    strength = jax.random.uniform(jax.random.fold_in(key, 13), (total_rows,), jnp.float32, 10.0, 25.0)
    shrink = 2.0 * math.sqrt(HEAD_SIZE) / (strength * HEAD_SIZE)
    final_keys = base_sample[:, FORK_STEPS - 1]
    early_keys = jnp.where(aligned[:, None], final_keys * (1.0 - shrink[:, None]), base_sample[:, 0])
    output_keys = jnp.concatenate([early_keys[:, None], base_sample[:, 1:]], axis=1)
    return (output_keys, aligned, strength)


def draw_decoded_keys(key, part):
    align_share = 0.0
    output_keys, aligned, strength = shared_keys(key, align_share)
    return output_keys.astype(jnp.bfloat16)


def draw_queries(key, part):
    align_share = 0.0
    output_keys, aligned, strength = shared_keys(key, align_share)
    key = jax.random.fold_in(key, 5)
    total_rows = REQUEST_FORKS * N_SECTION * N_EP
    grouped_heads = QUERY_HEADS // KEY_VALUE_HEADS
    random_noise = jnp.clip(jax.random.normal(key, (total_rows, FORK_STEPS, KEY_VALUE_HEADS, grouped_heads, HEAD_SIZE), jnp.float32), -4.0, 4.0)
    local_keys = jnp.broadcast_to(output_keys.reshape(total_rows, FORK_STEPS, KEY_VALUE_HEADS, 1, HEAD_SIZE), random_noise.shape)
    mixed = 0.5 * local_keys + random_noise
    pointed = strength[:, None, None, None] * local_keys[:, FORK_STEPS - 1]
    final_step = jnp.where(aligned[:, None, None, None], pointed, mixed[:, FORK_STEPS - 1])
    mixed = jnp.concatenate([mixed[:, :FORK_STEPS - 1], final_step[:, None]], axis=1)
    return mixed.reshape(total_rows, FORK_STEPS, QUERY_HEADS * HEAD_SIZE).astype(jnp.bfloat16)


def shard_levels(own_key, shape, split, least, high):
    def one(dim, parts):
        heights = jax.random.uniform(jax.random.fold_in(jax.random.fold_in(own_key, 6), dim), (parts,), jnp.float32, least / len(split), high / len(split))
        return jnp.repeat(jnp.exp(heights), shape[dim] // parts).reshape((-1,) + (1,) * (len(shape) - dim - 1))

    factor_of = one(*split[0])
    for cut in split[1:]:
        factor_of = factor_of * one(*cut)
    return factor_of


def routed_block(rng, own, number, rows, number_of, top, most, slope):
    order = jax.random.permutation(rng, number_of)
    packed, common = shares(number_of, rows * top, most, slope, True), shares(number_of, rows * top, most, slope, False)
    places = jnp.arange(number_of)

    def named(tallies, turn):
        used = int((tallies > 0).sum())
        fixed = max(1, used // 4)
        passed = fixed + (places - fixed + turn * (used - fixed)) % max(1, number_of - fixed)
        return jnp.zeros((number_of,), jnp.int32).at[order[jnp.where(places < fixed, places, passed)]].set(jnp.asarray(tallies, jnp.int32))

    tallies = jnp.where(number % 4 == 0, named(packed, number // 4), named(common, number - number // 4 - 1))
    mixed = jax.random.permutation(jax.random.fold_in(own, 3), number_of)
    donor, sink = mixed[0:number_of // 2 * 2:2], mixed[1:number_of // 2 * 2:2]
    slack = jnp.minimum(tallies[donor] - 1, most - tallies[sink]) // 2
    slack = jnp.where((donor == order[0]) | (sink == order[0]) | (tallies[sink] == 0), 0, jnp.maximum(slack, 0))
    passed = jax.random.randint(jax.random.fold_in(own, 4), (number_of // 2,), 0, 1 << 20) % (slack + 1)
    tallies = tallies.at[donor].add(-passed).at[sink].add(passed)
    members = jnp.searchsorted(jnp.cumsum(tallies), jnp.arange(rows * top), side="right").astype(jnp.int32)
    table = members.reshape(top, rows).T
    table = table[jax.random.permutation(jax.random.fold_in(own, 1), rows)]
    turn = jax.random.randint(jax.random.fold_in(own, 2), (rows, 1), 0, top)
    return jnp.take_along_axis(table, (jnp.arange(top)[None, :] + turn) % top, axis=1)


def shares(number_of, total, reach, skew, full):
    loads = [(1 << 20) // math.isqrt(rank ** skew) + 1 for rank in range(1, number_of + 1)]
    largest = reach if full else min(reach, max(-(-total // number_of), total * loads[0] // sum(loads)))
    least = 1 if total - largest >= number_of - 1 else 0
    given, surplus = [largest] + [least] * (number_of - 1), total - largest - least * (number_of - 1)
    while surplus > 0:
        candidates = [i for i in range(1, number_of) if given[i] < largest] or [i for i in range(1, number_of) if given[i] < reach]
        mass, left = sum([loads[i] for i in candidates]), surplus
        for i in candidates:
            more = min(reach - given[i], max(1, left * loads[i] // mass), surplus)
            given[i] = given[i] + more
            surplus = surplus - more
    return np.array(given)


def scatter_about(own_key, dims, deviation, bound, split=(), kind=jnp.bfloat16):
    drawn = jax.random.normal(own_key, dims, jnp.float32) * deviation
    if len(split) > 0:
        drawn = shard_levels(own_key, dims, split, -0.22, 0.18) * drawn
    return jnp.clip(drawn, min=-bound, max=bound).astype(kind)


def setup_inputs(seed: int = 0, part: int = 0) -> dict:
    splits = jax.random.split(jax.random.key(seed), 7)
    part_splits = jax.random.split(jax.random.fold_in(splits[6], part), 7)
    tokens = scatter_about(part_splits[0], (PROMPT_TOKENS, D), 1.0, 6.0, ((0, 8), (1, 2)))
    w_kv = scatter_about(splits[1], (D, KV_COLS), D ** -0.5, 0.078125, ((0, 8), (1, 2)))
    page_target_keys = jax.random.split(jax.random.fold_in(part_splits[2], 1), PAGES // PG_DEV)
    page_target_turns = jax.random.permutation(jax.random.fold_in(part_splits[2], 3), PAGES // PG_DEV)
    page_target = jax.vmap(lambda own, number: routed_block(jax.random.fold_in(part_splits[2], 2), own, number, PG_DEV, N_SECTION * N_EP, 1, CAP, 2))(page_target_keys, page_target_turns).reshape((PAGES, 1))
    queries = draw_queries(jax.random.fold_in(jax.random.fold_in(splits[6], part), 71), part)
    decoded_keys = draw_decoded_keys(jax.random.fold_in(jax.random.fold_in(splits[6], part), 71), part)
    decoded_values = scatter_about(part_splits[5], (TOTAL_FORKS, FORK_STEPS, KEY_VALUE_HEADS * HEAD_SIZE), 1.0, 6.0, ((0, 8), (2, 2)))
    return {"tokens": tokens, "w_kv": w_kv, "page_target": page_target, "queries": queries, "decoded_keys": decoded_keys, "decoded_values": decoded_values}


def reference(tokens, w_kv, page_target, queries, decoded_keys, decoded_values):
    projected_rows = jnp.dot(tokens, w_kv, preferred_element_type=jnp.float32).astype(jnp.bfloat16)
    projected_rows = projected_rows.reshape(PROMPT_TOKENS, KEY_VALUE_HEADS, 2, HEAD_SIZE)
    prompt_keys = projected_rows[:, :, 0].astype(jnp.float32)
    prompt_values = projected_rows[:, :, 1].astype(jnp.float32)
    token_request = jnp.repeat(page_target[:, 0], PAGE)
    grouped_heads = QUERY_HEADS // KEY_VALUE_HEADS
    inv_root = 1.0 / math.sqrt(HEAD_SIZE)
    causal = jnp.arange(FORK_STEPS)[None, :] <= jnp.arange(FORK_STEPS)[:, None]

    def one_request(request):
        leading_fork = (request * REQUEST_FORKS).astype(jnp.int32)
        query_head_list = lax.dynamic_slice_in_dim(queries, leading_fork, REQUEST_FORKS, 0).astype(jnp.float32)
        query_head_list = query_head_list.reshape(REQUEST_FORKS, FORK_STEPS, KEY_VALUE_HEADS, grouped_heads, HEAD_SIZE)
        latest_keys = lax.dynamic_slice_in_dim(decoded_keys, leading_fork, REQUEST_FORKS, 0).astype(jnp.float32).reshape(REQUEST_FORKS, FORK_STEPS, KEY_VALUE_HEADS, HEAD_SIZE)
        latest_values = lax.dynamic_slice_in_dim(decoded_values, leading_fork, REQUEST_FORKS, 0).astype(jnp.float32).reshape(REQUEST_FORKS, FORK_STEPS, KEY_VALUE_HEADS, HEAD_SIZE)
        live = token_request == request
        prompt_scores = jnp.einsum('fsgjd,tgd->gfsjt', query_head_list, prompt_keys) * inv_root
        prompt_scores = jnp.where(live, prompt_scores, -jnp.inf)
        fresh_scores = jnp.einsum('fsgjd,fugd->gfsju', query_head_list, latest_keys) * inv_root
        fresh_scores = jnp.where(causal[None, None, :, None, :], fresh_scores, -jnp.inf)
        peak_score = jnp.maximum(lax.optimization_barrier(jnp.max(prompt_scores, -1)), lax.optimization_barrier(jnp.max(fresh_scores, -1)))[..., None]
        prompt_exp = jnp.exp(prompt_scores - peak_score)
        fresh_exp = jnp.exp(fresh_scores - peak_score)
        normalizer = lax.optimization_barrier(jnp.sum(prompt_exp, -1, keepdims=True)) + lax.optimization_barrier(jnp.sum(fresh_exp, -1, keepdims=True))
        prompt_weights = (prompt_exp / normalizer).astype(jnp.bfloat16).astype(jnp.float32)
        fresh_weights = (fresh_exp / normalizer).astype(jnp.bfloat16).astype(jnp.float32)
        combined = jnp.einsum('gfsjt,tgd->fsgjd', prompt_weights, prompt_values)
        combined = combined + jnp.einsum('gfsju,fugd->fsgjd', fresh_weights, latest_values)
        return combined.reshape(REQUEST_FORKS, FORK_STEPS, QUERY_HEADS * HEAD_SIZE).astype(jnp.bfloat16)
    outputs = lax.map(one_request, jnp.arange(N_SECTION * N_EP, dtype=jnp.int32))
    return outputs.reshape(TOTAL_FORKS, FORK_STEPS, QUERY_HEADS * HEAD_SIZE)
```

```python
import functools
import math

import jax
import jax.numpy as jnp
from jax import lax
from jax.experimental import pallas as pl
from jax.experimental.pallas import tpu as pltpu
from jax.sharding import PartitionSpec as P

QUERY_HEADS = 48
KEY_VALUE_HEADS = 8
HEAD_SIZE = 128
PAGE = 16
MESH = pl.DeviceIdType.MESH
CHUNKS = 4
CHUNK = 256
ROW_TILE = 256


def project_kernel(nz, tok, w, out, wbuf, csend, crecv, own, xs, rown, zs, zr, ys, yr, cs, cr, ps, pr):
    x = lax.axis_index("tp")
    y = lax.axis_index("groups")
    z = lax.axis_index("ep")
    k = lax.axis_index("section")
    q = 2 * y + k
    rows = tok.shape[0]
    depth = tok.shape[1]
    steps = 2 * CHUNKS

    barrier = pltpu.get_barrier_semaphore()
    for dz in range(1, nz):
        pl.semaphore_signal(barrier, inc=1, device_id={"ep": lax.rem(z + dz, nz)}, device_id_type=MESH)
    pl.semaphore_signal(barrier, inc=1, device_id={"groups": 1 - y}, device_id_type=MESH)
    pl.semaphore_signal(barrier, inc=1, device_id={"section": 1 - k}, device_id_type=MESH)
    for c in range(2):
        pl.semaphore_signal(barrier, inc=1, device_id={"tp": 1 - x, "section": c}, device_id_type=MESH)
    pl.semaphore_wait(barrier, nz + 3)

    def x_copy(j, c):
        cols = pl.ds(pl.multiple_of(j * CHUNK, CHUNK), CHUNK)
        return pltpu.make_async_remote_copy(
            src_ref=w.at[2 * y + c, :, cols], dst_ref=wbuf.at[j, z, 2 * y + c],
            send_sem=xs.at[j, c], recv_sem=rown.at[j],
            device_id={"tp": 1 - x, "section": c}, device_id_type=MESH)

    def peer_copy(j):
        cols = pl.ds(pl.multiple_of(j * CHUNK, CHUNK), CHUNK)
        return pltpu.make_async_remote_copy(
            src_ref=w.at[2 * y + 1 - k, :, cols], dst_ref=wbuf.at[CHUNKS + j, z, 2 * y + 1 - k],
            send_sem=xs.at[j, 0], recv_sem=rown.at[CHUNKS + j],
            device_id={"section": 1 - k}, device_id_type=MESH)

    def local_copy(j):
        cols = pl.ds(pl.multiple_of(j * CHUNK, CHUNK), CHUNK)
        return pltpu.make_async_copy(w.at[q, :, cols], wbuf.at[CHUNKS + j, z, q], rown.at[CHUNKS + j])

    def own_wait(e):
        return pltpu.make_async_remote_copy(
            src_ref=wbuf.at[e, z, q], dst_ref=wbuf.at[e, z, q],
            send_sem=xs.at[0, 0], recv_sem=rown.at[e],
            device_id={"section": 1 - k}, device_id_type=MESH)

    def z_copy(e, dz):
        return pltpu.make_async_remote_copy(
            src_ref=wbuf.at[e, z, q], dst_ref=wbuf.at[e, z, q],
            send_sem=zs.at[e, dz - 1], recv_sem=zr.at[e, dz - 1],
            device_id={"ep": lax.rem(z + dz, nz)}, device_id_type=MESH)

    def z_wait(e, dz):
        src = lax.rem(z + nz - dz, nz)
        return pltpu.make_async_remote_copy(
            src_ref=wbuf.at[e, src, q], dst_ref=wbuf.at[e, src, q],
            send_sem=zs.at[e, dz - 1], recv_sem=zr.at[e, dz - 1],
            device_id={"ep": src}, device_id_type=MESH)

    def y_copy(e, part):
        return pltpu.make_async_remote_copy(
            src_ref=wbuf.at[e, :, part], dst_ref=wbuf.at[e, :, part],
            send_sem=ys.at[e], recv_sem=yr.at[e],
            device_id={"groups": 1 - y}, device_id_type=MESH)

    def core_copy(e, side, part):
        return pltpu.make_async_remote_copy(
            src_ref=wbuf.at[e, :, part], dst_ref=wbuf.at[e, :, part],
            send_sem=cs.at[e, side], recv_sem=cr.at[e, side],
            device_id={"section": 1 - k}, device_id_type=MESH)

    def part_copy(j):
        return pltpu.make_async_remote_copy(
            src_ref=csend.at[j], dst_ref=crecv.at[j],
            send_sem=ps.at[j], recv_sem=pr.at[j],
            device_id={"tp": 1 - x}, device_id_type=MESH)

    @pl.when(k != x)
    def _():
        for j in range(CHUNKS):
            x_copy(j, 0).start()
            x_copy(j, 1).start()

    @pl.when(k == x)
    def _():
        for j in range(CHUNKS):
            peer_copy(j).start()
            local_copy(j).start()

    def multiply(e, tile):
        at = pl.ds(pl.multiple_of(tile * ROW_TILE, ROW_TILE), ROW_TILE)
        product = jnp.dot(tok[at, :], wbuf[e].reshape(depth, CHUNK), preferred_element_type=jnp.float32)
        return at, product

    def step(i, carry):
        @pl.when(i < steps)
        def _():
            e = i

            @pl.when((e < CHUNKS) | (k != x))
            def _():
                own_wait(e).wait_recv()

            @pl.when((e >= CHUNKS) & (k == x))
            def _():
                local_copy(e - CHUNKS).wait()

            for dz in range(1, nz):
                z_copy(e, dz).start()

        @pl.when((i >= 2) & (i < steps + 2))
        def _():
            e = i - 2
            for dz in range(1, nz):
                z_wait(e, dz).wait_recv()
            y_copy(e, q).start()
            core_copy(e, 0, q).start()

        @pl.when((i >= 4) & (i < steps + 4))
        def _():
            e = i - 4
            other = 2 * (1 - y) + k
            y_copy(e, other).wait_recv()
            core_copy(e, 1, other).start()

        @pl.when(i >= 5)
        def _():
            e = i - 5
            core_copy(e, 0, 2 * y + 1 - k).wait_recv()
            core_copy(e, 1, 2 * (1 - y) + 1 - k).wait_recv()

            @pl.when(e < CHUNKS)
            def _():
                def body(tile, c):
                    at, product = multiply(e, tile)
                    csend[e, at, :] = product.astype(jnp.bfloat16)
                    return c
                lax.fori_loop(0, rows // ROW_TILE, body, 0)
                part_copy(e).start()

            @pl.when(e >= CHUNKS)
            def _():
                def body(tile, c):
                    at, product = multiply(e, tile)
                    own[e - CHUNKS, at, :] = product
                    return c
                lax.fori_loop(0, rows // ROW_TILE, body, 0)

        return carry

    lax.fori_loop(0, steps + 5, step, 0)
    for j in range(CHUNKS):
        part_copy(j).wait_recv()
        out[:, j * CHUNK:(j + 1) * CHUNK] = (own[j] + crecv[j].astype(jnp.float32)).astype(jnp.bfloat16)

    @pl.when(k != x)
    def _():
        for j in range(CHUNKS):
            x_copy(j, 0).wait_send()
            x_copy(j, 1).wait_send()

    @pl.when(k == x)
    def _():
        for j in range(CHUNKS):
            peer_copy(j).wait_send()

    def drain(e, carry):
        for dz in range(1, nz):
            z_copy(e, dz).wait_send()
        y_copy(e, q).wait_send()
        core_copy(e, 0, q).wait_send()
        core_copy(e, 1, 2 * (1 - y) + k).wait_send()
        return carry

    lax.fori_loop(0, steps, drain, 0)
    for j in range(CHUNKS):
        part_copy(j).wait_send()


def project(tokens, w_kv):
    nz = lax.axis_size("ep")
    rows, depth = tokens.shape
    w_rows, width = w_kv.shape
    quarter = w_rows // 4
    steps = 2 * CHUNKS
    dma = pltpu.SemaphoreType.DMA
    vmem = pl.BlockSpec(memory_space=pltpu.VMEM)
    return pl.pallas_call(
        functools.partial(project_kernel, nz),
        out_shape=jax.ShapeDtypeStruct((rows, width), jnp.bfloat16),
        in_specs=[vmem, vmem],
        out_specs=vmem,
        scratch_shapes=[
            pltpu.VMEM((steps, nz, 4, quarter, CHUNK), jnp.bfloat16),
            pltpu.VMEM((CHUNKS, rows, CHUNK), jnp.bfloat16),
            pltpu.VMEM((CHUNKS, rows, CHUNK), jnp.bfloat16),
            pltpu.VMEM((CHUNKS, rows, CHUNK), jnp.float32),
            dma((CHUNKS, 2)),
            dma((steps,)),
            dma((steps, nz - 1)),
            dma((steps, nz - 1)),
            dma((steps,)),
            dma((steps,)),
            dma((steps, 2)),
            dma((steps, 2)),
            dma((CHUNKS,)),
            dma((CHUNKS,)),
        ],
        compiler_params=pltpu.CompilerParams(
            collective_id=0, has_side_effects=True, vmem_limit_bytes=56 << 20),
        cost_estimate=pl.CostEstimate(
            flops=4 * rows * depth * width, bytes_accessed=16 << 20, transcendentals=0),
        name="project",
    )(tokens, w_kv.reshape(4, quarter, width))


def local(tokens, w_kv, page_target, queries, decoded_keys, decoded_values):
    kv_width = w_kv.shape[1]
    if (lax.axis_size("groups"), lax.axis_size("section"), lax.axis_size("tp")) == (2, 2, 2):
        projected_rows = project(tokens, w_kv)
    else:
        projected_rows = jnp.dot(
            lax.all_gather(tokens, "tp", axis=1, tiled=True),
            lax.all_gather(w_kv, ("section", "ep"), axis=0, tiled=True),
            preferred_element_type=jnp.float32,
        )
    page_rows = tokens.shape[0] // PAGE
    page_data = projected_rows.astype(jnp.bfloat16).reshape(page_rows, PAGE * kv_width)
    targets = page_target[:, 0]
    dest_count = lax.axis_size(("section", "ep"))
    capacity = max(2, 2 * page_rows // dest_count)
    same_target = targets[:, None] == targets[None, :]
    earlier = jnp.arange(page_rows)[None, :] < jnp.arange(page_rows)[:, None]
    ranks = jnp.sum((same_target & earlier).astype(jnp.int32), axis=1)
    slot_index = targets * capacity + ranks
    placed = slot_index[None, :] == jnp.arange(dest_count * capacity, dtype=jnp.int32)[:, None]
    outgoing = jnp.dot(
        placed.astype(jnp.bfloat16), page_data, preferred_element_type=jnp.float32
    ).astype(jnp.bfloat16)
    filled = jnp.sum(placed.astype(jnp.int32), axis=1)
    arrived, live_slots = (
        lax.all_to_all(
            outgoing.reshape(dest_count, capacity, PAGE, kv_width),
            ("section", "ep"),
            split_axis=0,
            concat_axis=0,
            tiled=True,
        ),
        lax.all_to_all(
            filled.reshape(dest_count, capacity),
            ("section", "ep"),
            split_axis=0,
            concat_axis=0,
            tiled=True,
        ),
    )
    head_pairs = kv_width // (2 * HEAD_SIZE)
    arrived = arrived.reshape(-1, head_pairs, 2, HEAD_SIZE)
    prompt_keys = arrived[:, :, 0]
    prompt_values = arrived[:, :, 1]
    slot_live = jnp.repeat(live_slots.reshape(-1), PAGE) > 0
    forks = queries.shape[0]
    steps = queries.shape[1]
    grouped_heads = QUERY_HEADS // KEY_VALUE_HEADS
    query_head_list = queries.reshape(forks, steps, head_pairs, grouped_heads, HEAD_SIZE)
    latest_keys = decoded_keys.reshape(forks, steps, head_pairs, HEAD_SIZE)
    latest_values = decoded_values.reshape(forks, steps, head_pairs, HEAD_SIZE)
    inv_root = 1.0 / math.sqrt(HEAD_SIZE)
    prompt_scores = (
        jnp.einsum(
            "fsgjd,tgd->gfsjt", query_head_list, prompt_keys, preferred_element_type=jnp.float32
        )
        * inv_root
    )
    prompt_scores = jnp.where(slot_live, prompt_scores, -jnp.inf)
    fresh_scores = (
        jnp.einsum(
            "fsgjd,fugd->gfsju", query_head_list, latest_keys, preferred_element_type=jnp.float32
        )
        * inv_root
    )
    causal = jnp.arange(steps)[None, :] <= jnp.arange(steps)[:, None]
    fresh_scores = jnp.where(causal[None, None, :, None, :], fresh_scores, -jnp.inf)
    peak_score = jnp.maximum(jnp.max(prompt_scores, -1), jnp.max(fresh_scores, -1))[..., None]
    prompt_exp = jnp.exp(prompt_scores - peak_score)
    fresh_exp = jnp.exp(fresh_scores - peak_score)
    normalizer = jnp.sum(prompt_exp, -1, keepdims=True) + jnp.sum(fresh_exp, -1, keepdims=True)
    prompt_weights = (prompt_exp / normalizer).astype(jnp.bfloat16)
    fresh_weights = (fresh_exp / normalizer).astype(jnp.bfloat16)
    combined = jnp.einsum(
        "gfsjt,tgd->fsgjd", prompt_weights, prompt_values, preferred_element_type=jnp.float32
    )
    combined = combined + jnp.einsum(
        "gfsju,fugd->fsgjd", fresh_weights, latest_values, preferred_element_type=jnp.float32
    )
    return combined.reshape(forks, steps, -1).astype(jnp.bfloat16)


def solution(mesh):
    in_specs = (
        P(("groups", "section", "ep"), "tp"),
        P(("section", "ep"), "tp"),
        P(("groups", "section", "ep"), None),
        P(("groups", "section", "ep"), None, "tp"),
        P(("groups", "section", "ep"), None, "tp"),
        P(("groups", "section", "ep"), None, "tp"),
    )
    out_specs = P(("groups", "section", "ep"), None, "tp")
    return jax.shard_map(local, mesh=mesh, in_specs=in_specs, out_specs=out_specs, check_vma=False)
```

```python
import functools
import math

import jax
import jax.numpy as jnp
from jax import lax
from jax.experimental import pallas as pl
from jax.experimental.pallas import tpu as pltpu
from jax.sharding import PartitionSpec as P

QUERY_HEADS = 48
KEY_VALUE_HEADS = 8
HEAD_SIZE = 128
PAGE = 16
STEPS = 2
GROUPED = QUERY_HEADS // KEY_VALUE_HEADS
MESH = pl.DeviceIdType.MESH
CHUNKS = 4
HALF = CHUNKS // 2
CHUNK = 2 * HEAD_SIZE
ROW_TILE = 256
LOG2E = math.log2(math.e)
NEVER = -1e30


def serve_kernel(nz, tok, w, requests, qown, fresh_k, fresh_v, out, wbuf, csend, crecv, own, qall, po, pst, cpo, cpst,
                 zo, zst, ro, rst, fo, fst, xs, rown, zs, zr, ys, yr, cs, cr, ps, pr,
                 qs, qr, qcs, qcr, hs, hr, gs, gr, fs, fr):
    x = lax.axis_index("tp")
    y = lax.axis_index("groups")
    z = lax.axis_index("ep")
    k = lax.axis_index("section")
    q = 2 * y + k
    rows = tok.shape[0]
    depth = tok.shape[1]
    steps = 2 * CHUNKS

    barrier = pltpu.get_barrier_semaphore()
    for dz in range(1, nz):
        pl.semaphore_signal(barrier, inc=1, device_id={"ep": lax.rem(z + dz, nz)}, device_id_type=MESH)
    pl.semaphore_signal(barrier, inc=1, device_id={"groups": 1 - y}, device_id_type=MESH)
    pl.semaphore_signal(barrier, inc=1, device_id={"section": 1 - k}, device_id_type=MESH)
    for c in range(2):
        pl.semaphore_signal(barrier, inc=1, device_id={"tp": 1 - x, "section": c}, device_id_type=MESH)
    pl.semaphore_wait(barrier, nz + 3)

    def x_copy(j, c):
        cols = pl.ds(pl.multiple_of(j * CHUNK, CHUNK), CHUNK)
        return pltpu.make_async_remote_copy(
            src_ref=w.at[2 * y + c, :, cols], dst_ref=wbuf.at[j, z, 2 * y + c],
            send_sem=xs.at[j, c], recv_sem=rown.at[j],
            device_id={"tp": 1 - x, "section": c}, device_id_type=MESH)

    def peer_copy(j):
        cols = pl.ds(pl.multiple_of(j * CHUNK, CHUNK), CHUNK)
        return pltpu.make_async_remote_copy(
            src_ref=w.at[2 * y + 1 - k, :, cols], dst_ref=wbuf.at[CHUNKS + j, z, 2 * y + 1 - k],
            send_sem=xs.at[j, 0], recv_sem=rown.at[CHUNKS + j],
            device_id={"section": 1 - k}, device_id_type=MESH)

    def local_copy(j):
        cols = pl.ds(pl.multiple_of(j * CHUNK, CHUNK), CHUNK)
        return pltpu.make_async_copy(w.at[q, :, cols], wbuf.at[CHUNKS + j, z, q], rown.at[CHUNKS + j])

    def own_wait(e):
        return pltpu.make_async_remote_copy(
            src_ref=wbuf.at[e, z, q], dst_ref=wbuf.at[e, z, q],
            send_sem=xs.at[0, 0], recv_sem=rown.at[e],
            device_id={"section": 1 - k}, device_id_type=MESH)

    def z_copy(e, dz):
        return pltpu.make_async_remote_copy(
            src_ref=wbuf.at[e, z, q], dst_ref=wbuf.at[e, z, q],
            send_sem=zs.at[e, dz - 1], recv_sem=zr.at[e, dz - 1],
            device_id={"ep": lax.rem(z + dz, nz)}, device_id_type=MESH)

    def z_wait(e, dz):
        src = lax.rem(z + nz - dz, nz)
        return pltpu.make_async_remote_copy(
            src_ref=wbuf.at[e, src, q], dst_ref=wbuf.at[e, src, q],
            send_sem=zs.at[e, dz - 1], recv_sem=zr.at[e, dz - 1],
            device_id={"ep": src}, device_id_type=MESH)

    def y_copy(e, part):
        return pltpu.make_async_remote_copy(
            src_ref=wbuf.at[e, :, part], dst_ref=wbuf.at[e, :, part],
            send_sem=ys.at[e], recv_sem=yr.at[e],
            device_id={"groups": 1 - y}, device_id_type=MESH)

    def core_copy(e, side, part):
        return pltpu.make_async_remote_copy(
            src_ref=wbuf.at[e, :, part], dst_ref=wbuf.at[e, :, part],
            send_sem=cs.at[e, side], recv_sem=cr.at[e, side],
            device_id={"section": 1 - k}, device_id_type=MESH)

    def part_copy(j):
        return pltpu.make_async_remote_copy(
            src_ref=csend.at[j], dst_ref=crecv.at[j],
            send_sem=ps.at[j], recv_sem=pr.at[j],
            device_id={"tp": 1 - x}, device_id_type=MESH)

    lanes = 2 * qown.shape[1]
    scale = LOG2E / math.sqrt(HEAD_SIZE)

    def q_copy(dz):
        return pltpu.make_async_remote_copy(
            src_ref=qown, dst_ref=qall.at[z, k], send_sem=qs.at[dz - 1], recv_sem=qr.at[dz - 1],
            device_id={"ep": lax.rem(z + dz, nz)}, device_id_type=MESH)

    def q_wait(dz):
        src = lax.rem(z + nz - dz, nz)
        return pltpu.make_async_remote_copy(
            src_ref=qown, dst_ref=qall.at[src, k], send_sem=qs.at[dz - 1], recv_sem=qr.at[dz - 1],
            device_id={"ep": src}, device_id_type=MESH)

    def q_core(core):
        return pltpu.make_async_remote_copy(
            src_ref=qall.at[:, core], dst_ref=qall.at[:, core], send_sem=qcs, recv_sem=qcr,
            device_id={"section": 1 - k}, device_id_type=MESH)

    def head_copies(j):
        return [pltpu.make_async_remote_copy(
            src_ref=a.at[j], dst_ref=b.at[j // 2], send_sem=hs.at[j // 2, n], recv_sem=hr.at[j // 2, n],
            device_id={"section": 1 - k}, device_id_type=MESH)
            for n, (a, b) in enumerate([(po, cpo), (pst, cpst)])]

    def chip_copies(jj, dz):
        to = lax.rem(z + dz, nz)
        return [pltpu.make_async_remote_copy(
            src_ref=a.at[jj, to], dst_ref=b.at[jj, z], send_sem=gs.at[jj, dz - 1, n], recv_sem=gr.at[jj, dz - 1, n],
            device_id={"ep": to}, device_id_type=MESH)
            for n, (a, b) in enumerate([(zo, ro), (zst, rst)])]

    def chip_waits(jj, dz):
        src = lax.rem(z + nz - dz, nz)
        return [pltpu.make_async_remote_copy(
            src_ref=a.at[jj, src], dst_ref=b.at[jj, src], send_sem=gs.at[jj, dz - 1, n],
            recv_sem=gr.at[jj, dz - 1, n], device_id={"ep": src}, device_id_type=MESH)
            for n, (a, b) in enumerate([(zo, ro), (zst, rst)])]

    def final_copies(jj, core):
        return [pltpu.make_async_remote_copy(
            src_ref=a.at[core, jj], dst_ref=a.at[core, jj], send_sem=fs.at[jj, n], recv_sem=fr.at[jj, n],
            device_id={"section": 1 - k}, device_id_type=MESH)
            for n, a in enumerate([fo, fst])]

    def attend(j, keys, values):
        lane = lax.broadcasted_iota(jnp.int32, (1, lanes), 1)
        lane_core = (lane >= lanes // 2).astype(jnp.int32)
        values_t = values.T

        def body(block, carry):
            heads = qall[block, :, j].reshape(lanes, HEAD_SIZE)
            scores = lax.dot_general(keys, heads, (((1,), (1,)), ((), ())), preferred_element_type=jnp.float32)
            mine = requests[...] == lane_core * nz + block
            scores = jnp.where(mine, scores * scale, NEVER)
            peak = jnp.max(scores, axis=0, keepdims=True)
            weights = jnp.exp2(scores - peak)
            total = jnp.sum(weights, axis=0, keepdims=True)
            sums = jnp.dot(values_t, weights.astype(jnp.bfloat16), preferred_element_type=jnp.float32)
            po[j, block] = sums.astype(jnp.bfloat16)
            pst[j, block, 0:1] = peak
            pst[j, block, 1:2] = total
            return carry

        lax.fori_loop(0, nz, body, 0)

    def merge(items):
        peak = items[0][1]
        for item in items[1:]:
            peak = jnp.maximum(peak, item[1])
        factors = [jnp.exp2(item[1] - peak) for item in items]
        total = sum(f * item[2] for f, item in zip(factors, items))
        sums = sum(f * item[0].astype(jnp.float32) for f, item in zip(factors, items))
        return sums, peak, total

    def combine_cores(j):
        jj = j // 2

        @pl.when(k == j % 2)
        def _():
            for c in head_copies(j):
                c.wait_recv()
            for b in range(nz):
                sums, peak, total = merge([
                    (po[j, b], pst[j, b, 0:1], pst[j, b, 1:2]),
                    (cpo[jj, b], cpst[jj, b, 0:1], cpst[jj, b, 1:2])])
                zo[jj, b] = sums.astype(jnp.bfloat16)
                zst[jj, b, 0:1] = peak
                zst[jj, b, 1:2] = total
            for dz in range(1, nz):
                for c in chip_copies(jj, dz):
                    c.start()

    def combine_chips(jj):
        items = [(zo[jj, z], zst[jj, z, 0:1], zst[jj, z, 1:2])]
        for dz in range(1, nz):
            for c in chip_waits(jj, dz):
                c.wait_recv()
            src = lax.rem(z + nz - dz, nz)
            items.append((ro[jj, src], rst[jj, src, 0:1], rst[jj, src, 1:2]))
        sums, peak, total = merge(items)
        fo[k, jj] = sums.T
        fst[k, jj, 0] = jnp.broadcast_to(peak, (HEAD_SIZE, lanes)).T
        fst[k, jj, 1] = jnp.broadcast_to(total, (HEAD_SIZE, lanes)).T

    def finish(j):
        rows_of = pl.ds(pl.multiple_of(k * (lanes // 2), 64), lanes // 2)
        sums = fo[j % 2, j // 2, rows_of]
        peak = fst[j % 2, j // 2, 0, rows_of]
        total = fst[j % 2, j // 2, 1, rows_of]
        query = qown[j].astype(jnp.float32)
        row = lax.broadcasted_iota(jnp.int32, (lanes // 2, 1), 0)
        row_step = lax.rem(row // GROUPED, STEPS)
        fresh = []
        for u in range(STEPS):
            s = jnp.sum(query * fresh_k[u, j].astype(jnp.float32), axis=1, keepdims=True) * scale
            fresh.append(jnp.where(row_step >= u, s, NEVER))
        top = peak
        for s in fresh:
            top = jnp.maximum(top, s)
        fade = jnp.exp2(peak - top)
        exps = [jnp.exp2(s - top) for s in fresh]
        inverse = 1.0 / (fade * total + sum(exps))
        result = sums * (fade * inverse)
        for u in range(STEPS):
            weight = (exps[u] * inverse).astype(jnp.bfloat16).astype(jnp.float32)
            result = result + weight * fresh_v[u, j].astype(jnp.float32)
        out[j] = result.astype(jnp.bfloat16)

    @pl.when(k != x)
    def _():
        for j in range(CHUNKS):
            x_copy(j, 0).start()
            x_copy(j, 1).start()

    @pl.when(k == x)
    def _():
        for j in range(CHUNKS):
            peer_copy(j).start()
            local_copy(j).start()

    def multiply(e, tile):
        at = pl.ds(pl.multiple_of(tile * ROW_TILE, ROW_TILE), ROW_TILE)
        product = jnp.dot(tok[at, :], wbuf[e].reshape(depth, CHUNK), preferred_element_type=jnp.float32)
        return at, product

    qall[z, k] = qown[...]

    def step(i, carry):
        @pl.when(i < steps)
        def _():
            e = i

            @pl.when((e < CHUNKS) | (k != x))
            def _():
                own_wait(e).wait_recv()

            @pl.when((e >= CHUNKS) & (k == x))
            def _():
                local_copy(e - CHUNKS).wait()

            for dz in range(1, nz):
                z_copy(e, dz).start()

        @pl.when((i >= 2) & (i < steps + 2))
        def _():
            e = i - 2
            for dz in range(1, nz):
                z_wait(e, dz).wait_recv()
            y_copy(e, q).start()
            core_copy(e, 0, q).start()

        @pl.when(i == steps)
        def _():
            for dz in range(1, nz):
                q_copy(dz).start()

        @pl.when((i >= 4) & (i < steps + 4))
        def _():
            e = i - 4
            other = 2 * (1 - y) + k
            y_copy(e, other).wait_recv()
            core_copy(e, 1, other).start()

        @pl.when(i >= 5)
        def _():
            e = i - 5
            core_copy(e, 0, 2 * y + 1 - k).wait_recv()
            core_copy(e, 1, 2 * (1 - y) + 1 - k).wait_recv()

            @pl.when(e < CHUNKS)
            def _():
                def body(tile, c):
                    at, product = multiply(e, tile)
                    csend[e, at, :] = product.astype(jnp.bfloat16)
                    return c
                lax.fori_loop(0, rows // ROW_TILE, body, 0)
                part_copy(e).start()

            @pl.when(e >= CHUNKS)
            def _():
                def body(tile, c):
                    at, product = multiply(e, tile)
                    own[e - CHUNKS, at, :] = product
                    return c
                lax.fori_loop(0, rows // ROW_TILE, body, 0)

        return carry

    lax.fori_loop(0, steps + 5, step, 0)
    for dz in range(1, nz):
        q_wait(dz).wait_recv()
    q_core(k).start()
    q_core(1 - k).wait_recv()
    for j in range(CHUNKS):
        part_copy(j).wait_recv()
        block = (own[j] + crecv[j].astype(jnp.float32)).astype(jnp.bfloat16)
        keys, values = block[:, :HEAD_SIZE], block[:, HEAD_SIZE:]
        attend(j, keys, values)

        @pl.when(k != j % 2)
        def _():
            for c in head_copies(j):
                c.start()

        if j >= 1:
            combine_cores(j - 1)
    combine_cores(CHUNKS - 1)
    for jj in range(HALF):
        combine_chips(jj)
    for jj in range(HALF):
        for c in final_copies(jj, k):
            c.start()
    for j in range(CHUNKS):
        jj = j // 2

        @pl.when(k != j % 2)
        def _():
            for c in final_copies(jj, 1 - k):
                c.wait_recv()

        finish(j)

    @pl.when(k != x)
    def _():
        for j in range(CHUNKS):
            x_copy(j, 0).wait_send()
            x_copy(j, 1).wait_send()

    @pl.when(k == x)
    def _():
        for j in range(CHUNKS):
            peer_copy(j).wait_send()

    def drain(e, carry):
        for dz in range(1, nz):
            z_copy(e, dz).wait_send()
        y_copy(e, q).wait_send()
        core_copy(e, 0, q).wait_send()
        core_copy(e, 1, 2 * (1 - y) + k).wait_send()
        return carry

    lax.fori_loop(0, steps, drain, 0)
    for j in range(CHUNKS):
        part_copy(j).wait_send()

    for dz in range(1, nz):
        q_copy(dz).wait_send()
    q_core(k).wait_send()
    for j in range(CHUNKS):
        @pl.when(k != j % 2)
        def _():
            for c in head_copies(j):
                c.wait_send()
    for jj in range(HALF):
        for dz in range(1, nz):
            for c in chip_copies(jj, dz):
                c.wait_send()
        for c in final_copies(jj, k):
            c.wait_send()


def serve(tokens, w_kv, page_target, queries, decoded_keys, decoded_values):
    nz = lax.axis_size("ep")
    rows, depth = tokens.shape
    w_rows, width = w_kv.shape
    forks = queries.shape[0]
    quarter = w_rows // 4
    steps = 2 * CHUNKS
    q_rows = forks * STEPS * GROUPED
    lanes = 2 * q_rows
    qown = queries.reshape(forks, STEPS, CHUNKS, GROUPED, HEAD_SIZE)
    qown = qown.transpose(2, 0, 1, 3, 4).reshape(CHUNKS, q_rows, HEAD_SIZE)

    def spread(a):
        a = a.reshape(forks, STEPS, CHUNKS, 1, HEAD_SIZE).transpose(1, 2, 0, 3, 4)
        a = jnp.broadcast_to(a, (STEPS, CHUNKS, forks, STEPS * GROUPED, HEAD_SIZE))
        return a.reshape(STEPS, CHUNKS, q_rows, HEAD_SIZE)

    requests = jnp.repeat(page_target[:, 0], PAGE)[:, None]
    dma = pltpu.SemaphoreType.DMA
    vmem = pl.BlockSpec(memory_space=pltpu.VMEM)
    bf16, f32 = jnp.bfloat16, jnp.float32
    out = pl.pallas_call(
        functools.partial(serve_kernel, nz),
        out_shape=jax.ShapeDtypeStruct((CHUNKS, q_rows, HEAD_SIZE), bf16),
        in_specs=[vmem] * 6,
        out_specs=vmem,
        scratch_shapes=[
            pltpu.VMEM((steps, nz, 4, quarter, CHUNK), bf16),
            pltpu.VMEM((CHUNKS, rows, CHUNK), bf16),
            pltpu.VMEM((CHUNKS, rows, CHUNK), bf16),
            pltpu.VMEM((CHUNKS, rows, CHUNK), f32),
            pltpu.VMEM((nz, 2, CHUNKS, q_rows, HEAD_SIZE), bf16),
            pltpu.VMEM((CHUNKS, nz, HEAD_SIZE, lanes), bf16),
            pltpu.VMEM((CHUNKS, nz, 8, lanes), f32),
            pltpu.VMEM((HALF, nz, HEAD_SIZE, lanes), bf16),
            pltpu.VMEM((HALF, nz, 8, lanes), f32),
            pltpu.VMEM((HALF, nz, HEAD_SIZE, lanes), bf16),
            pltpu.VMEM((HALF, nz, 8, lanes), f32),
            pltpu.VMEM((HALF, nz, HEAD_SIZE, lanes), bf16),
            pltpu.VMEM((HALF, nz, 8, lanes), f32),
            pltpu.VMEM((2, HALF, lanes, HEAD_SIZE), f32),
            pltpu.VMEM((2, HALF, 2, lanes, HEAD_SIZE), f32),
            dma((CHUNKS, 2)), dma((steps,)),
            dma((steps, nz - 1)), dma((steps, nz - 1)),
            dma((steps,)), dma((steps,)),
            dma((steps, 2)), dma((steps, 2)),
            dma((CHUNKS,)), dma((CHUNKS,)),
            dma((nz - 1,)), dma((nz - 1,)), dma, dma,
            dma((HALF, 2)), dma((HALF, 2)),
            dma((HALF, nz - 1, 2)), dma((HALF, nz - 1, 2)),
            dma((HALF, 2)), dma((HALF, 2)),
        ],
        compiler_params=pltpu.CompilerParams(
            collective_id=0, has_side_effects=True, vmem_limit_bytes=60 << 20),
        cost_estimate=pl.CostEstimate(
            flops=4 * rows * depth * width, bytes_accessed=16 << 20, transcendentals=0),
        name="serve",
    )(tokens, w_kv.reshape(4, quarter, width), requests, qown, spread(decoded_keys), spread(decoded_values))
    out = out.reshape(CHUNKS, forks, STEPS, GROUPED, HEAD_SIZE).transpose(1, 2, 0, 3, 4)
    return out.reshape(forks, STEPS, CHUNKS * GROUPED * HEAD_SIZE)


def local(tokens, w_kv, page_target, queries, decoded_keys, decoded_values):
    axes = tuple(lax.axis_size(a) for a in ("groups", "section", "tp"))
    if axes == (2, 2, 2) and w_kv.shape[1] == CHUNKS * CHUNK:
        return serve(tokens, w_kv, page_target, queries, decoded_keys, decoded_values)
    gathered = lax.all_gather(tokens, "tp", axis=1, tiled=True)
    kv_width = w_kv.shape[1]
    projected_rows = jnp.dot(
        gathered,
        lax.all_gather(w_kv, ("section", "ep"), axis=0, tiled=True),
        preferred_element_type=jnp.float32,
    )
    page_rows = gathered.shape[0] // PAGE
    page_data = projected_rows.astype(jnp.bfloat16).reshape(page_rows, PAGE * kv_width)
    targets = page_target[:, 0]
    dest_count = lax.axis_size(("section", "ep"))
    capacity = max(2, 2 * page_rows // dest_count)
    same_target = targets[:, None] == targets[None, :]
    earlier = jnp.arange(page_rows)[None, :] < jnp.arange(page_rows)[:, None]
    ranks = jnp.sum((same_target & earlier).astype(jnp.int32), axis=1)
    slot_index = targets * capacity + ranks
    placed = slot_index[None, :] == jnp.arange(dest_count * capacity, dtype=jnp.int32)[:, None]
    outgoing = jnp.dot(
        placed.astype(jnp.bfloat16), page_data, preferred_element_type=jnp.float32
    ).astype(jnp.bfloat16)
    filled = jnp.sum(placed.astype(jnp.int32), axis=1)
    arrived, live_slots = (
        lax.all_to_all(
            outgoing.reshape(dest_count, capacity, PAGE, kv_width),
            ("section", "ep"),
            split_axis=0,
            concat_axis=0,
            tiled=True,
        ),
        lax.all_to_all(
            filled.reshape(dest_count, capacity),
            ("section", "ep"),
            split_axis=0,
            concat_axis=0,
            tiled=True,
        ),
    )
    head_pairs = kv_width // (2 * HEAD_SIZE)
    arrived = arrived.reshape(-1, head_pairs, 2, HEAD_SIZE)
    prompt_keys = arrived[:, :, 0]
    prompt_values = arrived[:, :, 1]
    slot_live = jnp.repeat(live_slots.reshape(-1), PAGE) > 0
    forks = queries.shape[0]
    steps = queries.shape[1]
    grouped_heads = QUERY_HEADS // KEY_VALUE_HEADS
    query_head_list = queries.reshape(forks, steps, head_pairs, grouped_heads, HEAD_SIZE)
    latest_keys = decoded_keys.reshape(forks, steps, head_pairs, HEAD_SIZE)
    latest_values = decoded_values.reshape(forks, steps, head_pairs, HEAD_SIZE)
    inv_root = 1.0 / math.sqrt(HEAD_SIZE)
    prompt_scores = (
        jnp.einsum(
            "fsgjd,tgd->gfsjt", query_head_list, prompt_keys, preferred_element_type=jnp.float32
        )
        * inv_root
    )
    prompt_scores = jnp.where(slot_live, prompt_scores, -jnp.inf)
    fresh_scores = (
        jnp.einsum(
            "fsgjd,fugd->gfsju", query_head_list, latest_keys, preferred_element_type=jnp.float32
        )
        * inv_root
    )
    causal = jnp.arange(steps)[None, :] <= jnp.arange(steps)[:, None]
    fresh_scores = jnp.where(causal[None, None, :, None, :], fresh_scores, -jnp.inf)
    peak_score = jnp.maximum(jnp.max(prompt_scores, -1), jnp.max(fresh_scores, -1))[..., None]
    prompt_exp = jnp.exp(prompt_scores - peak_score)
    fresh_exp = jnp.exp(fresh_scores - peak_score)
    normalizer = jnp.sum(prompt_exp, -1, keepdims=True) + jnp.sum(fresh_exp, -1, keepdims=True)
    prompt_weights = (prompt_exp / normalizer).astype(jnp.bfloat16)
    fresh_weights = (fresh_exp / normalizer).astype(jnp.bfloat16)
    combined = jnp.einsum(
        "gfsjt,tgd->fsgjd", prompt_weights, prompt_values, preferred_element_type=jnp.float32
    )
    combined = combined + jnp.einsum(
        "gfsju,fugd->fsgjd", fresh_weights, latest_values, preferred_element_type=jnp.float32
    )
    return combined.reshape(forks, steps, -1).astype(jnp.bfloat16)


def solution(mesh):
    in_specs = (
        P(("groups", "section", "ep"), "tp"),
        P(("section", "ep"), "tp"),
        P(("groups", "section", "ep"), None),
        P(("groups", "section", "ep"), None, "tp"),
        P(("groups", "section", "ep"), None, "tp"),
        P(("groups", "section", "ep"), None, "tp"),
    )
    out_specs = P(("groups", "section", "ep"), None, "tp")
    return jax.shard_map(local, mesh=mesh, in_specs=in_specs, out_specs=out_specs, check_vma=False)
```

```python
import functools
import math

import jax
import jax.numpy as jnp
from jax import lax
from jax.experimental import pallas as pl
from jax.experimental.pallas import tpu as pltpu
from jax.sharding import PartitionSpec as P

QUERY_HEADS = 48
KEY_VALUE_HEADS = 8
HEAD_SIZE = 128
PAGE = 16
STEPS = 2
GROUPED = QUERY_HEADS // KEY_VALUE_HEADS
MESH = pl.DeviceIdType.MESH
CHUNKS = 4
HALF = CHUNKS // 2
CHUNK = 2 * HEAD_SIZE
ROW_TILE = 256
LOG2E = math.log2(math.e)
NEVER = -1e30
AHEAD = 2
SKEW_Y = 3
SKEW_M = 3


def serve_kernel(nz, tok_hbm, w, requests, qown, fresh_k, fresh_v, out, tok, wbuf, csend, crecv, kv, qall, po, pst, cpo, cpst,
                 zo, zst, ro, rst, fo, fst, xs, rown, zs, zr, ys, yr, cs, cr, ps, pr,
                 qs, qr, qcs, qcr, hs, hr, gs, gr, fs, fr, ts):
    x = lax.axis_index("tp")
    y = lax.axis_index("groups")
    z = lax.axis_index("ep")
    k = lax.axis_index("section")
    q = 2 * y + k
    forks = fresh_k.shape[1]
    rows = tok.shape[0]
    depth = tok.shape[1]
    steps = 2 * CHUNKS

    barrier = pltpu.get_barrier_semaphore()
    for dz in range(1, nz):
        pl.semaphore_signal(barrier, inc=1, device_id={"ep": lax.rem(z + dz, nz)}, device_id_type=MESH)
    pl.semaphore_signal(barrier, inc=1, device_id={"groups": 1 - y}, device_id_type=MESH)
    pl.semaphore_signal(barrier, inc=1, device_id={"section": 1 - k}, device_id_type=MESH)
    for c in range(2):
        pl.semaphore_signal(barrier, inc=1, device_id={"tp": 1 - x, "section": c}, device_id_type=MESH)
    tok_copy = pltpu.make_async_copy(tok_hbm, tok, ts)
    tok_copy.start()
    pl.semaphore_wait(barrier, nz + 3)

    def x_copy(j, c):
        cols = pl.ds(pl.multiple_of(j * CHUNK, CHUNK), CHUNK)
        return pltpu.make_async_remote_copy(
            src_ref=w.at[2 * y + c, :, cols], dst_ref=wbuf.at[j, z, 2 * y + c],
            send_sem=xs.at[j, c], recv_sem=rown.at[j],
            device_id={"tp": 1 - x, "section": c}, device_id_type=MESH)

    def peer_copy(j):
        cols = pl.ds(pl.multiple_of(j * CHUNK, CHUNK), CHUNK)
        return pltpu.make_async_remote_copy(
            src_ref=w.at[:, :, cols], dst_ref=wbuf.at[CHUNKS + j, z],
            send_sem=xs.at[j, 0], recv_sem=rown.at[CHUNKS + j],
            device_id={"section": 1 - k}, device_id_type=MESH)

    def local_copy(j):
        cols = pl.ds(pl.multiple_of(j * CHUNK, CHUNK), CHUNK)
        return pltpu.make_async_copy(w.at[:, :, cols], wbuf.at[CHUNKS + j, z], rown.at[CHUNKS + j])

    def z_hop(e):
        def hop(src, right):
            block = wbuf.at[e, src, q]
            return pltpu.make_async_remote_copy(
                src_ref=block, dst_ref=block, send_sem=zs.at[e, src, right], recv_sem=zr.at[e, src],
                device_id={"ep": lax.rem(z + 1 if right else z + nz - 1, nz)}, device_id_type=MESH)
        return hop

    def q_hop(src, right):
        block = qall.at[src, k]
        return pltpu.make_async_remote_copy(
            src_ref=block, dst_ref=block, send_sem=qs.at[src, right], recv_sem=qr.at[src],
            device_id={"ep": lax.rem(z + 1 if right else z + nz - 1, nz)}, device_id_type=MESH)

    def send_own(hop):
        @pl.when(z < nz - 1)
        def _():
            hop(z, 1).start()

        @pl.when(z > 0)
        def _():
            hop(z, 0).start()

    def pass_on(hop, d, then):
        @pl.when(z - d >= 0)
        def _():
            hop(z - d, 1).wait_recv()

            @pl.when(z < nz - 1)
            def _():
                hop(z - d, 1).start()
            then(z - d)

        @pl.when(z + d < nz)
        def _():
            hop(z + d, 0).wait_recv()

            @pl.when(z > 0)
            def _():
                hop(z + d, 0).start()
            then(z + d)

    def drain_hops(hop):
        @pl.when(z < nz - 1)
        def _():
            hop(z, 1).wait_send()

        @pl.when(z > 0)
        def _():
            hop(z, 0).wait_send()

        for d in range(1, nz):
            @pl.when((z - d >= 0) & (z < nz - 1))
            def _():
                hop(z - d, 1).wait_send()

            @pl.when((z + d < nz) & (z > 0))
            def _():
                hop(z + d, 0).wait_send()

    def y_copy(e, src, part):
        return pltpu.make_async_remote_copy(
            src_ref=wbuf.at[e, src, part], dst_ref=wbuf.at[e, src, part],
            send_sem=ys.at[e, src], recv_sem=yr.at[e, src],
            device_id={"groups": 1 - y}, device_id_type=MESH)

    def core_copy(e, side, src, part):
        return pltpu.make_async_remote_copy(
            src_ref=wbuf.at[e, src, part], dst_ref=wbuf.at[e, src, part],
            send_sem=cs.at[e, side, src], recv_sem=cr.at[e, side, src],
            device_id={"section": 1 - k}, device_id_type=MESH)

    def share(e, src):
        y_copy(e, src, q).start()
        core_copy(e, 0, src, q).start()

    def each_source(e, what):
        for d in range(nz):
            src = lax.rem(z + d, nz)
            if d == 0:
                @pl.when(e < CHUNKS)
                def _():
                    what(src)
            else:
                what(src)

    def part_copy(j):
        return pltpu.make_async_remote_copy(
            src_ref=csend.at[j], dst_ref=crecv.at[j],
            send_sem=ps.at[j], recv_sem=pr.at[j],
            device_id={"tp": 1 - x}, device_id_type=MESH)

    lanes = 2 * qown.shape[1]
    scale = LOG2E / math.sqrt(HEAD_SIZE)

    def q_core(core):
        return pltpu.make_async_remote_copy(
            src_ref=qall.at[:, core], dst_ref=qall.at[:, core], send_sem=qcs, recv_sem=qcr,
            device_id={"section": 1 - k}, device_id_type=MESH)

    def head_copies(j):
        return [pltpu.make_async_remote_copy(
            src_ref=a.at[j], dst_ref=b.at[lax.div(j, 2)], send_sem=hs.at[lax.div(j, 2), n],
            recv_sem=hr.at[lax.div(j, 2), n],
            device_id={"section": 1 - k}, device_id_type=MESH)
            for n, (a, b) in enumerate([(po, cpo), (pst, cpst)])]

    def chip_copies(jj, dz):
        to = lax.rem(z + dz, nz)
        return [pltpu.make_async_remote_copy(
            src_ref=a.at[jj, to], dst_ref=b.at[jj, z], send_sem=gs.at[jj, dz - 1, n], recv_sem=gr.at[jj, dz - 1, n],
            device_id={"ep": to}, device_id_type=MESH)
            for n, (a, b) in enumerate([(zo, ro), (zst, rst)])]

    def chip_waits(jj, dz):
        src = lax.rem(z + nz - dz, nz)
        return [pltpu.make_async_remote_copy(
            src_ref=a.at[jj, src], dst_ref=b.at[jj, src], send_sem=gs.at[jj, dz - 1, n],
            recv_sem=gr.at[jj, dz - 1, n], device_id={"ep": src}, device_id_type=MESH)
            for n, (a, b) in enumerate([(zo, ro), (zst, rst)])]

    def final_copies(jj, core):
        return [pltpu.make_async_remote_copy(
            src_ref=a.at[core, jj], dst_ref=a.at[core, jj], send_sem=fs.at[jj, n], recv_sem=fr.at[jj, n],
            device_id={"section": 1 - k}, device_id_type=MESH)
            for n, a in enumerate([fo, fst])]

    def attend(j):
        lane = lax.broadcasted_iota(jnp.int32, (1, lanes), 1)
        lane_core = (lane >= lanes // 2).astype(jnp.int32)
        keys = kv[:, :HEAD_SIZE]
        values_t = kv[:, HEAD_SIZE:].T

        def body(block, carry):
            heads = qall[block, :, j].reshape(lanes, HEAD_SIZE)
            scores = lax.dot_general(keys, heads, (((1,), (1,)), ((), ())), preferred_element_type=jnp.float32)
            mine = requests[...] == lane_core * nz + block
            scores = jnp.where(mine, scores * scale, NEVER)
            peak = jnp.max(scores, axis=0, keepdims=True)
            weights = jnp.exp2(scores - peak)
            total = jnp.sum(weights, axis=0, keepdims=True)
            sums = jnp.dot(values_t, weights.astype(jnp.bfloat16), preferred_element_type=jnp.float32)
            po[j, block] = sums.astype(jnp.bfloat16)
            pst[j, block, 0:1] = peak
            pst[j, block, 1:2] = total
            return carry

        lax.fori_loop(0, nz, body, 0)

    def merge(items):
        peak = items[0][1]
        for item in items[1:]:
            peak = jnp.maximum(peak, item[1])
        factors = [jnp.exp2(item[1] - peak) for item in items]
        total = sum(f * item[2] for f, item in zip(factors, items))
        sums = sum(f * item[0].astype(jnp.float32) for f, item in zip(factors, items))
        return sums, peak, total

    def combine_cores(j):
        jj = lax.div(j, 2)

        @pl.when(k == lax.rem(j, 2))
        def _():
            for c in head_copies(j):
                c.wait_recv()
            for b in range(nz):
                sums, peak, total = merge([
                    (po[j, b], pst[j, b, 0:1], pst[j, b, 1:2]),
                    (cpo[jj, b], cpst[jj, b, 0:1], cpst[jj, b, 1:2])])
                zo[jj, b] = sums.astype(jnp.bfloat16)
                zst[jj, b, 0:1] = peak
                zst[jj, b, 1:2] = total
            for dz in range(1, nz):
                for c in chip_copies(jj, dz):
                    c.start()

    def combine_chips(jj):
        items = [(zo[jj, z], zst[jj, z, 0:1], zst[jj, z, 1:2])]
        for dz in range(1, nz):
            for c in chip_waits(jj, dz):
                c.wait_recv()
            src = lax.rem(z + nz - dz, nz)
            items.append((ro[jj, src], rst[jj, src, 0:1], rst[jj, src, 1:2]))
        sums, peak, total = merge(items)
        fo[k, jj] = sums.T
        fst[k, jj, 0] = jnp.broadcast_to(peak, (HEAD_SIZE, lanes)).T
        fst[k, jj, 1] = jnp.broadcast_to(total, (HEAD_SIZE, lanes)).T

    def finish(j):
        rows_of = pl.ds(pl.multiple_of(k * (lanes // 2), 64), lanes // 2)
        sums = fo[j % 2, j // 2, rows_of]
        peak = fst[j % 2, j // 2, 0, rows_of]
        total = fst[j % 2, j // 2, 1, rows_of]
        query = qown[j].astype(jnp.float32)
        row = lax.broadcasted_iota(jnp.int32, (lanes // 2, 1), 0)
        row_step = lax.rem(row // forks, STEPS)
        head = slice(j * HEAD_SIZE, (j + 1) * HEAD_SIZE)
        copies = lanes // 2 // forks
        fresh = []
        for u in range(STEPS):
            latest = jnp.concatenate([fresh_k[u, :, head].astype(jnp.float32)] * copies, axis=0)
            s = jnp.sum(query * latest, axis=1, keepdims=True) * scale
            fresh.append(jnp.where(row_step >= u, s, NEVER))
        top = peak
        for s in fresh:
            top = jnp.maximum(top, s)
        fade = jnp.exp2(peak - top)
        exps = [jnp.exp2(s - top) for s in fresh]
        inverse = 1.0 / (fade * total + sum(exps))
        result = sums * (fade * inverse)
        for u in range(STEPS):
            weight = (exps[u] * inverse).astype(jnp.bfloat16).astype(jnp.float32)
            latest = jnp.concatenate([fresh_v[u, :, head].astype(jnp.float32)] * copies, axis=0)
            result = result + weight * latest
        out[j] = result.astype(jnp.bfloat16)

    @pl.when(k != x)
    def _():
        for j in range(CHUNKS):
            x_copy(j, 0).start()
            x_copy(j, 1).start()

    @pl.when(k == x)
    def _():
        for j in range(CHUNKS):
            peer_copy(j).start()
            local_copy(j).start()

    def multiply(e, tile):
        at = pl.ds(pl.multiple_of(tile * ROW_TILE, ROW_TILE), ROW_TILE)
        product = jnp.dot(tok[at, :], wbuf[e].reshape(depth, CHUNK), preferred_element_type=jnp.float32)
        return at, product

    qall[z, k] = qown[...]

    def begin(e):
        @pl.when(e < CHUNKS)
        def _():
            block = wbuf.at[e, z, q]
            pltpu.make_async_remote_copy(
                src_ref=block, dst_ref=block, send_sem=xs.at[0, 0], recv_sem=rown.at[e],
                device_id={"section": 1 - k}, device_id_type=MESH).wait_recv()
            send_own(z_hop(e))
            share(e, z)

        @pl.when(e >= CHUNKS)
        def _():
            @pl.when(k != x)
            def _():
                peer_copy(e - CHUNKS).wait_recv()

            @pl.when(k == x)
            def _():
                local_copy(e - CHUNKS).wait()

            send_own(z_hop(e))

    for e in range(AHEAD):
        begin(jnp.int32(e))
    tok_copy.wait()

    def own_head(j):
        part_copy(j).wait_recv()

        def body(tile, c):
            at, product = multiply(CHUNKS + j, tile)
            kv[at, :] = (product + crecv[j, at, :].astype(jnp.float32)).astype(jnp.bfloat16)
            return c
        lax.fori_loop(0, rows // ROW_TILE, body, 0)

        @pl.when(j == 0)
        def _():
            q_core(1 - k).wait_recv()

        attend(j)

        @pl.when(k != lax.rem(j, 2))
        def _():
            for c in head_copies(j):
                c.start()

        @pl.when(j >= 1)
        def _():
            combine_cores(j - 1)

    def step(i, carry):
        @pl.when(i + AHEAD < steps)
        def _():
            begin(i + AHEAD)

        @pl.when(i == 1)
        def _():
            send_own(q_hop)

        for d in range(1, nz):
            @pl.when((i >= d - 1) & (i < steps + d - 1))
            def _():
                e = i - (d - 1)
                pass_on(z_hop(e), d, functools.partial(share, e))

            @pl.when(i == d + 1)
            def _():
                pass_on(q_hop, d, lambda src: None)

        @pl.when(i == nz)
        def _():
            q_core(k).start()

        @pl.when((i >= SKEW_Y) & (i < steps + SKEW_Y))
        def _():
            e = i - SKEW_Y
            other = 2 * (1 - y) + k

            def forward(src):
                y_copy(e, src, other).wait_recv()
                core_copy(e, 1, src, other).start()
            each_source(e, forward)

        @pl.when(i >= SKEW_M)
        def _():
            e = i - SKEW_M

            def arrive(src):
                core_copy(e, 0, src, 2 * y + 1 - k).wait_recv()
                core_copy(e, 1, src, 2 * (1 - y) + 1 - k).wait_recv()
            each_source(e, arrive)

            @pl.when(e < CHUNKS)
            def _():
                def body(tile, c):
                    at, product = multiply(e, tile)
                    csend[e, at, :] = product.astype(jnp.bfloat16)
                    return c
                lax.fori_loop(0, rows // ROW_TILE, body, 0)
                part_copy(e).start()

            @pl.when(e >= CHUNKS)
            def _():
                own_head(e - CHUNKS)

        return carry

    lax.fori_loop(0, steps + SKEW_M, step, 0)
    combine_cores(jnp.int32(CHUNKS - 1))
    for jj in range(HALF):
        combine_chips(jj)
        for c in final_copies(jj, k):
            c.start()
    for j in range(CHUNKS):
        jj = j // 2

        @pl.when(k != j % 2)
        def _():
            for c in final_copies(jj, 1 - k):
                c.wait_recv()

        finish(j)

    @pl.when(k != x)
    def _():
        for j in range(CHUNKS):
            x_copy(j, 0).wait_send()
            x_copy(j, 1).wait_send()

    @pl.when(k == x)
    def _():
        for j in range(CHUNKS):
            peer_copy(j).wait_send()

    def drain(e, carry):
        drain_hops(z_hop(e))

        def sent(src):
            y_copy(e, src, q).wait_send()
            core_copy(e, 0, src, q).wait_send()
            core_copy(e, 1, src, 2 * (1 - y) + k).wait_send()
        each_source(e, sent)
        return carry

    lax.fori_loop(0, steps, drain, 0)
    for j in range(CHUNKS):
        part_copy(j).wait_send()

    drain_hops(q_hop)
    q_core(k).wait_send()
    for j in range(CHUNKS):
        @pl.when(k != j % 2)
        def _():
            for c in head_copies(jnp.int32(j)):
                c.wait_send()
    for jj in range(HALF):
        for dz in range(1, nz):
            for c in chip_copies(jj, dz):
                c.wait_send()
        for c in final_copies(jj, k):
            c.wait_send()


def serve(tokens, w_kv, page_target, queries, decoded_keys, decoded_values):
    nz = lax.axis_size("ep")
    rows, depth = tokens.shape
    w_rows, width = w_kv.shape
    forks = queries.shape[0]
    quarter = w_rows // 4
    steps = 2 * CHUNKS
    q_rows = forks * STEPS * GROUPED
    lanes = 2 * q_rows
    qown = queries.reshape(forks, STEPS, CHUNKS, GROUPED, HEAD_SIZE)
    qown = qown.transpose(2, 3, 1, 0, 4).reshape(CHUNKS, q_rows, HEAD_SIZE)

    requests = jnp.repeat(page_target[:, 0], PAGE)[:, None]
    dma = pltpu.SemaphoreType.DMA
    vmem = pl.BlockSpec(memory_space=pltpu.VMEM)
    bf16, f32 = jnp.bfloat16, jnp.float32
    out = pl.pallas_call(
        functools.partial(serve_kernel, nz),
        out_shape=jax.ShapeDtypeStruct((CHUNKS, q_rows, HEAD_SIZE), bf16),
        in_specs=[pl.BlockSpec(memory_space=pl.ANY)] * 2 + [vmem] * 4,
        out_specs=vmem,
        scratch_shapes=[
            pltpu.VMEM((rows, depth), bf16),
            pltpu.VMEM((steps, nz, 4, quarter, CHUNK), bf16),
            pltpu.VMEM((CHUNKS, rows, CHUNK), bf16),
            pltpu.VMEM((CHUNKS, rows, CHUNK), bf16),
            pltpu.VMEM((rows, CHUNK), bf16),
            pltpu.VMEM((nz, 2, CHUNKS, q_rows, HEAD_SIZE), bf16),
            pltpu.VMEM((CHUNKS, nz, HEAD_SIZE, lanes), bf16),
            pltpu.VMEM((CHUNKS, nz, 8, lanes), f32),
            pltpu.VMEM((HALF, nz, HEAD_SIZE, lanes), bf16),
            pltpu.VMEM((HALF, nz, 8, lanes), f32),
            pltpu.VMEM((HALF, nz, HEAD_SIZE, lanes), bf16),
            pltpu.VMEM((HALF, nz, 8, lanes), f32),
            pltpu.VMEM((HALF, nz, HEAD_SIZE, lanes), bf16),
            pltpu.VMEM((HALF, nz, 8, lanes), f32),
            pltpu.VMEM((2, HALF, lanes, HEAD_SIZE), f32),
            pltpu.VMEM((2, HALF, 2, lanes, HEAD_SIZE), f32),
            dma((CHUNKS, 2)), dma((steps,)),
            dma((steps, nz, 2)), dma((steps, nz)),
            dma((steps, nz)), dma((steps, nz)),
            dma((steps, 2, nz)), dma((steps, 2, nz)),
            dma((CHUNKS,)), dma((CHUNKS,)),
            dma((nz, 2)), dma((nz,)), dma, dma,
            dma((HALF, 2)), dma((HALF, 2)),
            dma((HALF, nz - 1, 2)), dma((HALF, nz - 1, 2)),
            dma((HALF, 2)), dma((HALF, 2)), dma,
        ],
        compiler_params=pltpu.CompilerParams(
            collective_id=0, has_side_effects=True, vmem_limit_bytes=60 << 20),
        cost_estimate=pl.CostEstimate(
            flops=4 * rows * depth * width, bytes_accessed=16 << 20, transcendentals=0),
        name="serve",
    )(tokens, w_kv.reshape(4, quarter, width), requests, qown, decoded_keys.transpose(1, 0, 2), decoded_values.transpose(1, 0, 2))
    out = out.reshape(CHUNKS, GROUPED, STEPS, forks, HEAD_SIZE).transpose(3, 2, 0, 1, 4)
    return out.reshape(forks, STEPS, CHUNKS * GROUPED * HEAD_SIZE)


def local(tokens, w_kv, page_target, queries, decoded_keys, decoded_values):
    axes = tuple(lax.axis_size(a) for a in ("groups", "section", "tp"))
    if axes == (2, 2, 2) and w_kv.shape[1] == CHUNKS * CHUNK:
        return serve(tokens, w_kv, page_target, queries, decoded_keys, decoded_values)
    gathered = lax.all_gather(tokens, "tp", axis=1, tiled=True)
    kv_width = w_kv.shape[1]
    projected_rows = jnp.dot(
        gathered,
        lax.all_gather(w_kv, ("section", "ep"), axis=0, tiled=True),
        preferred_element_type=jnp.float32,
    )
    page_rows = gathered.shape[0] // PAGE
    page_data = projected_rows.astype(jnp.bfloat16).reshape(page_rows, PAGE * kv_width)
    targets = page_target[:, 0]
    dest_count = lax.axis_size(("section", "ep"))
    capacity = max(2, 2 * page_rows // dest_count)
    same_target = targets[:, None] == targets[None, :]
    earlier = jnp.arange(page_rows)[None, :] < jnp.arange(page_rows)[:, None]
    ranks = jnp.sum((same_target & earlier).astype(jnp.int32), axis=1)
    slot_index = targets * capacity + ranks
    placed = slot_index[None, :] == jnp.arange(dest_count * capacity, dtype=jnp.int32)[:, None]
    outgoing = jnp.dot(
        placed.astype(jnp.bfloat16), page_data, preferred_element_type=jnp.float32
    ).astype(jnp.bfloat16)
    filled = jnp.sum(placed.astype(jnp.int32), axis=1)
    arrived, live_slots = (
        lax.all_to_all(
            outgoing.reshape(dest_count, capacity, PAGE, kv_width),
            ("section", "ep"),
            split_axis=0,
            concat_axis=0,
            tiled=True,
        ),
        lax.all_to_all(
            filled.reshape(dest_count, capacity),
            ("section", "ep"),
            split_axis=0,
            concat_axis=0,
            tiled=True,
        ),
    )
    head_pairs = kv_width // (2 * HEAD_SIZE)
    arrived = arrived.reshape(-1, head_pairs, 2, HEAD_SIZE)
    prompt_keys = arrived[:, :, 0]
    prompt_values = arrived[:, :, 1]
    slot_live = jnp.repeat(live_slots.reshape(-1), PAGE) > 0
    forks = queries.shape[0]
    steps = queries.shape[1]
    grouped_heads = QUERY_HEADS // KEY_VALUE_HEADS
    query_head_list = queries.reshape(forks, steps, head_pairs, grouped_heads, HEAD_SIZE)
    latest_keys = decoded_keys.reshape(forks, steps, head_pairs, HEAD_SIZE)
    latest_values = decoded_values.reshape(forks, steps, head_pairs, HEAD_SIZE)
    inv_root = 1.0 / math.sqrt(HEAD_SIZE)
    prompt_scores = (
        jnp.einsum(
            "fsgjd,tgd->gfsjt", query_head_list, prompt_keys, preferred_element_type=jnp.float32
        )
        * inv_root
    )
    prompt_scores = jnp.where(slot_live, prompt_scores, -jnp.inf)
    fresh_scores = (
        jnp.einsum(
            "fsgjd,fugd->gfsju", query_head_list, latest_keys, preferred_element_type=jnp.float32
        )
        * inv_root
    )
    causal = jnp.arange(steps)[None, :] <= jnp.arange(steps)[:, None]
    fresh_scores = jnp.where(causal[None, None, :, None, :], fresh_scores, -jnp.inf)
    peak_score = jnp.maximum(jnp.max(prompt_scores, -1), jnp.max(fresh_scores, -1))[..., None]
    prompt_exp = jnp.exp(prompt_scores - peak_score)
    fresh_exp = jnp.exp(fresh_scores - peak_score)
    normalizer = jnp.sum(prompt_exp, -1, keepdims=True) + jnp.sum(fresh_exp, -1, keepdims=True)
    prompt_weights = (prompt_exp / normalizer).astype(jnp.bfloat16)
    fresh_weights = (fresh_exp / normalizer).astype(jnp.bfloat16)
    combined = jnp.einsum(
        "gfsjt,tgd->fsgjd", prompt_weights, prompt_values, preferred_element_type=jnp.float32
    )
    combined = combined + jnp.einsum(
        "gfsju,fugd->fsgjd", fresh_weights, latest_values, preferred_element_type=jnp.float32
    )
    return combined.reshape(forks, steps, -1).astype(jnp.bfloat16)


def solution(mesh):
    in_specs = (
        P(("groups", "section", "ep"), "tp"),
        P(("section", "ep"), "tp"),
        P(("groups", "section", "ep"), None),
        P(("groups", "section", "ep"), None, "tp"),
        P(("groups", "section", "ep"), None, "tp"),
        P(("groups", "section", "ep"), None, "tp"),
    )
    out_specs = P(("groups", "section", "ep"), None, "tp")
    return jax.shard_map(local, mesh=mesh, in_specs=in_specs, out_specs=out_specs, check_vma=False)
```

```python
import functools
import math

import jax
import jax.numpy as jnp
from jax import lax
from jax.experimental import pallas as pl
from jax.experimental.pallas import tpu as pltpu
from jax.sharding import PartitionSpec as P

QUERY_HEADS = 48
KEY_VALUE_HEADS = 8
HEAD_SIZE = 128
PAGE = 16
STEPS = 2
GROUPED = QUERY_HEADS // KEY_VALUE_HEADS
MESH = pl.DeviceIdType.MESH
CHUNKS = 4
HALF = CHUNKS // 2
CHUNK = 2 * HEAD_SIZE
ROW_TILE = 256
LOG2E = math.log2(math.e)
NEVER = -1e30
AHEAD = 1
SKEW_Y = 3
SKEW_M = 3


def serve_kernel(nz, tok_hbm, w, requests, qown, fresh_k, fresh_v, out, tok, wbuf, csend, crecv, kv, qall, po, pst, cpo, cpst,
                 zo, zst, ro, rst, fo, fst, xs, rown, zs, zr, ys, yr, cs, cr, ps, pr,
                 qs, qr, qcs, qcr, hs, hr, gs, gr, fs, fr, ts):
    x = lax.axis_index("tp")
    y = lax.axis_index("groups")
    z = lax.axis_index("ep")
    k = lax.axis_index("section")
    q = 2 * y + k
    forks = fresh_k.shape[1]
    rows = tok.shape[0]
    depth = tok.shape[1]
    steps = 2 * CHUNKS

    barrier = pltpu.get_barrier_semaphore()
    for dz in range(1, nz):
        pl.semaphore_signal(barrier, inc=1, device_id={"ep": lax.rem(z + dz, nz)}, device_id_type=MESH)
    pl.semaphore_signal(barrier, inc=1, device_id={"groups": 1 - y}, device_id_type=MESH)
    pl.semaphore_signal(barrier, inc=1, device_id={"section": 1 - k}, device_id_type=MESH)
    for c in range(2):
        pl.semaphore_signal(barrier, inc=1, device_id={"tp": 1 - x, "section": c}, device_id_type=MESH)
    tok_copy = pltpu.make_async_copy(tok_hbm, tok, ts)
    tok_copy.start()
    pl.semaphore_wait(barrier, nz + 3)

    def x_copy(j, c):
        cols = pl.ds(pl.multiple_of(j * CHUNK, CHUNK), CHUNK)
        return pltpu.make_async_remote_copy(
            src_ref=w.at[2 * y + c, :, cols], dst_ref=wbuf.at[j, z, 2 * y + c],
            send_sem=xs.at[j, c], recv_sem=rown.at[j],
            device_id={"tp": 1 - x, "section": c}, device_id_type=MESH)

    def peer_copy(j):
        cols = pl.ds(pl.multiple_of(j * CHUNK, CHUNK), CHUNK)
        return pltpu.make_async_remote_copy(
            src_ref=w.at[:, :, cols], dst_ref=wbuf.at[CHUNKS + j, z],
            send_sem=xs.at[j, 0], recv_sem=rown.at[CHUNKS + j],
            device_id={"section": 1 - k}, device_id_type=MESH)

    def local_copy(j):
        cols = pl.ds(pl.multiple_of(j * CHUNK, CHUNK), CHUNK)
        return pltpu.make_async_copy(w.at[:, :, cols], wbuf.at[CHUNKS + j, z], rown.at[CHUNKS + j])

    def z_hop(e):
        def hop(src, right):
            block = wbuf.at[e, src, q]
            return pltpu.make_async_remote_copy(
                src_ref=block, dst_ref=block, send_sem=zs.at[e, src, right], recv_sem=zr.at[e, src],
                device_id={"ep": lax.rem(z + 1 if right else z + nz - 1, nz)}, device_id_type=MESH)
        return hop

    def q_hop(src, right):
        block = qall.at[src, k]
        return pltpu.make_async_remote_copy(
            src_ref=block, dst_ref=block, send_sem=qs.at[src, right], recv_sem=qr.at[src],
            device_id={"ep": lax.rem(z + 1 if right else z + nz - 1, nz)}, device_id_type=MESH)

    def send_own(hop):
        @pl.when(z < nz - 1)
        def _():
            hop(z, 1).start()

        @pl.when(z > 0)
        def _():
            hop(z, 0).start()

    def pass_on(hop, d, then):
        @pl.when(z - d >= 0)
        def _():
            hop(z - d, 1).wait_recv()

            @pl.when(z < nz - 1)
            def _():
                hop(z - d, 1).start()
            then(z - d)

        @pl.when(z + d < nz)
        def _():
            hop(z + d, 0).wait_recv()

            @pl.when(z > 0)
            def _():
                hop(z + d, 0).start()
            then(z + d)

    def drain_hops(hop):
        @pl.when(z < nz - 1)
        def _():
            hop(z, 1).wait_send()

        @pl.when(z > 0)
        def _():
            hop(z, 0).wait_send()

        for d in range(1, nz):
            @pl.when((z - d >= 0) & (z < nz - 1))
            def _():
                hop(z - d, 1).wait_send()

            @pl.when((z + d < nz) & (z > 0))
            def _():
                hop(z + d, 0).wait_send()

    def y_copy(e, src, part):
        return pltpu.make_async_remote_copy(
            src_ref=wbuf.at[e, src, part], dst_ref=wbuf.at[e, src, part],
            send_sem=ys.at[e, src], recv_sem=yr.at[e, src],
            device_id={"groups": 1 - y}, device_id_type=MESH)

    def core_copy(e, side, src, part):
        return pltpu.make_async_remote_copy(
            src_ref=wbuf.at[e, src, part], dst_ref=wbuf.at[e, src, part],
            send_sem=cs.at[e, side, src], recv_sem=cr.at[e, side, src],
            device_id={"section": 1 - k}, device_id_type=MESH)

    def share(e, src):
        y_copy(e, src, q).start()
        core_copy(e, 0, src, q).start()

    def each_source(e, what):
        for d in range(nz):
            src = lax.rem(z + d, nz)
            if d == 0:
                @pl.when(e < CHUNKS)
                def _():
                    what(src)
            else:
                what(src)

    def part_copy(j):
        return pltpu.make_async_remote_copy(
            src_ref=csend.at[j], dst_ref=crecv.at[j],
            send_sem=ps.at[j], recv_sem=pr.at[j],
            device_id={"tp": 1 - x}, device_id_type=MESH)

    lanes = 2 * qown.shape[1]
    scale = LOG2E / math.sqrt(HEAD_SIZE)

    def q_core(core):
        return pltpu.make_async_remote_copy(
            src_ref=qall.at[:, core], dst_ref=qall.at[:, core], send_sem=qcs, recv_sem=qcr,
            device_id={"section": 1 - k}, device_id_type=MESH)

    def head_copies(j):
        return [pltpu.make_async_remote_copy(
            src_ref=a.at[j], dst_ref=b.at[lax.div(j, 2)], send_sem=hs.at[lax.div(j, 2), n],
            recv_sem=hr.at[lax.div(j, 2), n],
            device_id={"section": 1 - k}, device_id_type=MESH)
            for n, (a, b) in enumerate([(po, cpo), (pst, cpst)])]

    def chip_copies(jj, dz):
        to = lax.rem(z + dz, nz)
        return [pltpu.make_async_remote_copy(
            src_ref=a.at[jj, to], dst_ref=b.at[jj, z], send_sem=gs.at[jj, dz - 1, n], recv_sem=gr.at[jj, dz - 1, n],
            device_id={"ep": to}, device_id_type=MESH)
            for n, (a, b) in enumerate([(zo, ro), (zst, rst)])]

    def chip_waits(jj, dz):
        src = lax.rem(z + nz - dz, nz)
        return [pltpu.make_async_remote_copy(
            src_ref=a.at[jj, src], dst_ref=b.at[jj, src], send_sem=gs.at[jj, dz - 1, n],
            recv_sem=gr.at[jj, dz - 1, n], device_id={"ep": src}, device_id_type=MESH)
            for n, (a, b) in enumerate([(zo, ro), (zst, rst)])]

    def final_copies(jj, core):
        return [pltpu.make_async_remote_copy(
            src_ref=a.at[core, jj], dst_ref=a.at[core, jj], send_sem=fs.at[jj, n], recv_sem=fr.at[jj, n],
            device_id={"section": 1 - k}, device_id_type=MESH)
            for n, a in enumerate([fo, fst])]

    def attend(j):
        lane = lax.broadcasted_iota(jnp.int32, (1, lanes), 1)
        lane_core = (lane >= lanes // 2).astype(jnp.int32)
        keys = kv[:, :HEAD_SIZE]
        values_t = kv[:, HEAD_SIZE:].T

        def body(block, carry):
            heads = qall[block, :, j].reshape(lanes, HEAD_SIZE)
            scores = lax.dot_general(keys, heads, (((1,), (1,)), ((), ())), preferred_element_type=jnp.float32)
            mine = requests[...] == lane_core * nz + block
            scores = jnp.where(mine, scores * scale, NEVER)
            peak = jnp.max(scores, axis=0, keepdims=True)
            weights = jnp.exp2(scores - peak)
            total = jnp.sum(weights, axis=0, keepdims=True)
            sums = jnp.dot(values_t, weights.astype(jnp.bfloat16), preferred_element_type=jnp.float32)
            po[j, block] = sums.astype(jnp.bfloat16)
            pst[j, block, 0:1] = peak
            pst[j, block, 1:2] = total
            return carry

        lax.fori_loop(0, nz, body, 0)

    def merge(items):
        peak = items[0][1]
        for item in items[1:]:
            peak = jnp.maximum(peak, item[1])
        factors = [jnp.exp2(item[1] - peak) for item in items]
        total = sum(f * item[2] for f, item in zip(factors, items))
        sums = sum(f * item[0].astype(jnp.float32) for f, item in zip(factors, items))
        return sums, peak, total

    def combine_cores(j):
        jj = lax.div(j, 2)

        @pl.when(k == lax.rem(j, 2))
        def _():
            for c in head_copies(j):
                c.wait_recv()
            for b in range(nz):
                sums, peak, total = merge([
                    (po[j, b], pst[j, b, 0:1], pst[j, b, 1:2]),
                    (cpo[jj, b], cpst[jj, b, 0:1], cpst[jj, b, 1:2])])
                zo[jj, b] = sums.astype(jnp.bfloat16)
                zst[jj, b, 0:1] = peak
                zst[jj, b, 1:2] = total
            for dz in range(1, nz):
                for c in chip_copies(jj, dz):
                    c.start()

    def combine_chips(jj):
        items = [(zo[jj, z], zst[jj, z, 0:1], zst[jj, z, 1:2])]
        for dz in range(1, nz):
            for c in chip_waits(jj, dz):
                c.wait_recv()
            src = lax.rem(z + nz - dz, nz)
            items.append((ro[jj, src], rst[jj, src, 0:1], rst[jj, src, 1:2]))
        sums, peak, total = merge(items)
        fo[k, jj] = sums.T
        fst[k, jj, 0] = jnp.broadcast_to(peak, (HEAD_SIZE, lanes)).T
        fst[k, jj, 1] = jnp.broadcast_to(total, (HEAD_SIZE, lanes)).T

    def finish(j):
        rows_of = pl.ds(pl.multiple_of(k * (lanes // 2), 64), lanes // 2)
        sums = fo[j % 2, j // 2, rows_of]
        peak = fst[j % 2, j // 2, 0, rows_of]
        total = fst[j % 2, j // 2, 1, rows_of]
        query = qown[j].astype(jnp.float32)
        row = lax.broadcasted_iota(jnp.int32, (lanes // 2, 1), 0)
        row_step = lax.rem(row // forks, STEPS)
        head = slice(j * HEAD_SIZE, (j + 1) * HEAD_SIZE)
        copies = lanes // 2 // forks
        fresh = []
        for u in range(STEPS):
            latest = jnp.concatenate([fresh_k[u, :, head].astype(jnp.float32)] * copies, axis=0)
            s = jnp.sum(query * latest, axis=1, keepdims=True) * scale
            fresh.append(jnp.where(row_step >= u, s, NEVER))
        top = peak
        for s in fresh:
            top = jnp.maximum(top, s)
        fade = jnp.exp2(peak - top)
        exps = [jnp.exp2(s - top) for s in fresh]
        inverse = 1.0 / (fade * total + sum(exps))
        result = sums * (fade * inverse)
        for u in range(STEPS):
            weight = (exps[u] * inverse).astype(jnp.bfloat16).astype(jnp.float32)
            latest = jnp.concatenate([fresh_v[u, :, head].astype(jnp.float32)] * copies, axis=0)
            result = result + weight * latest
        out[j] = result.astype(jnp.bfloat16)

    @pl.when(k != x)
    def _():
        for j in range(CHUNKS):
            x_copy(j, 0).start()
            x_copy(j, 1).start()

    @pl.when(k == x)
    def _():
        for j in range(CHUNKS):
            peer_copy(j).start()
            local_copy(j).start()

    def multiply(e, tile):
        at = pl.ds(pl.multiple_of(tile * ROW_TILE, ROW_TILE), ROW_TILE)
        product = jnp.dot(tok[at, :], wbuf[e].reshape(depth, CHUNK), preferred_element_type=jnp.float32)
        return at, product

    qall[z, k] = qown[...]

    def begin(e):
        @pl.when(e < CHUNKS)
        def _():
            block = wbuf.at[e, z, q]
            pltpu.make_async_remote_copy(
                src_ref=block, dst_ref=block, send_sem=xs.at[0, 0], recv_sem=rown.at[e],
                device_id={"section": 1 - k}, device_id_type=MESH).wait_recv()
            send_own(z_hop(e))
            share(e, z)

        @pl.when(e >= CHUNKS)
        def _():
            @pl.when(k != x)
            def _():
                peer_copy(e - CHUNKS).wait_recv()

            @pl.when(k == x)
            def _():
                local_copy(e - CHUNKS).wait()

            send_own(z_hop(e))

    for e in range(AHEAD):
        begin(jnp.int32(e))
    tok_copy.wait()

    def own_head(j):
        part_copy(j).wait_recv()

        def body(tile, c):
            at, product = multiply(CHUNKS + j, tile)
            kv[at, :] = (product + crecv[j, at, :].astype(jnp.float32)).astype(jnp.bfloat16)
            return c
        lax.fori_loop(0, rows // ROW_TILE, body, 0)

        @pl.when(j == 0)
        def _():
            q_core(1 - k).wait_recv()

        attend(j)

        @pl.when(k != lax.rem(j, 2))
        def _():
            for c in head_copies(j):
                c.start()

        @pl.when(j >= 1)
        def _():
            combine_cores(j - 1)

    def step(i, carry):
        @pl.when(i + AHEAD < steps)
        def _():
            begin(i + AHEAD)

        @pl.when(i == 1)
        def _():
            send_own(q_hop)

        for d in range(1, nz):
            @pl.when((i >= d - 1) & (i < steps + d - 1))
            def _():
                e = i - (d - 1)
                pass_on(z_hop(e), d, functools.partial(share, e))

            @pl.when(i == d + 1)
            def _():
                pass_on(q_hop, d, lambda src: None)

        @pl.when(i == nz)
        def _():
            q_core(k).start()

        @pl.when((i >= SKEW_Y) & (i < steps + SKEW_Y))
        def _():
            e = i - SKEW_Y
            other = 2 * (1 - y) + k

            def forward(src):
                y_copy(e, src, other).wait_recv()
                core_copy(e, 1, src, other).start()
            each_source(e, forward)

        @pl.when(i >= SKEW_M)
        def _():
            e = i - SKEW_M

            def arrive(src):
                core_copy(e, 0, src, 2 * y + 1 - k).wait_recv()
                core_copy(e, 1, src, 2 * (1 - y) + 1 - k).wait_recv()
            each_source(e, arrive)

            @pl.when(e < CHUNKS)
            def _():
                def body(tile, c):
                    at, product = multiply(e, tile)
                    csend[e, at, :] = product.astype(jnp.bfloat16)
                    return c
                lax.fori_loop(0, rows // ROW_TILE, body, 0)
                part_copy(e).start()

            @pl.when(e >= CHUNKS)
            def _():
                own_head(e - CHUNKS)

        return carry

    lax.fori_loop(0, steps + SKEW_M, step, 0)
    combine_cores(jnp.int32(CHUNKS - 1))
    for jj in range(HALF):
        combine_chips(jj)
        for c in final_copies(jj, k):
            c.start()
    for j in range(CHUNKS):
        jj = j // 2

        @pl.when(k != j % 2)
        def _():
            for c in final_copies(jj, 1 - k):
                c.wait_recv()

        finish(j)

    @pl.when(k != x)
    def _():
        for j in range(CHUNKS):
            x_copy(j, 0).wait_send()
            x_copy(j, 1).wait_send()

    @pl.when(k == x)
    def _():
        for j in range(CHUNKS):
            peer_copy(j).wait_send()

    def drain(e, carry):
        drain_hops(z_hop(e))

        def sent(src):
            y_copy(e, src, q).wait_send()
            core_copy(e, 0, src, q).wait_send()
            core_copy(e, 1, src, 2 * (1 - y) + k).wait_send()
        each_source(e, sent)
        return carry

    lax.fori_loop(0, steps, drain, 0)
    for j in range(CHUNKS):
        part_copy(j).wait_send()

    drain_hops(q_hop)
    q_core(k).wait_send()
    for j in range(CHUNKS):
        @pl.when(k != j % 2)
        def _():
            for c in head_copies(jnp.int32(j)):
                c.wait_send()
    for jj in range(HALF):
        for dz in range(1, nz):
            for c in chip_copies(jj, dz):
                c.wait_send()
        for c in final_copies(jj, k):
            c.wait_send()


def serve(tokens, w_kv, page_target, queries, decoded_keys, decoded_values):
    nz = lax.axis_size("ep")
    rows, depth = tokens.shape
    w_rows, width = w_kv.shape
    forks = queries.shape[0]
    quarter = w_rows // 4
    steps = 2 * CHUNKS
    q_rows = forks * STEPS * GROUPED
    lanes = 2 * q_rows
    qown = queries.reshape(forks, STEPS, CHUNKS, GROUPED, HEAD_SIZE)
    qown = qown.transpose(2, 3, 1, 0, 4).reshape(CHUNKS, q_rows, HEAD_SIZE)

    requests = jnp.repeat(page_target[:, 0], PAGE)[:, None]
    dma = pltpu.SemaphoreType.DMA
    vmem = pl.BlockSpec(memory_space=pltpu.VMEM)
    bf16, f32 = jnp.bfloat16, jnp.float32
    out = pl.pallas_call(
        functools.partial(serve_kernel, nz),
        out_shape=jax.ShapeDtypeStruct((CHUNKS, q_rows, HEAD_SIZE), bf16),
        in_specs=[pl.BlockSpec(memory_space=pl.ANY)] * 2 + [vmem] * 4,
        out_specs=vmem,
        scratch_shapes=[
            pltpu.VMEM((rows, depth), bf16),
            pltpu.VMEM((steps, nz, 4, quarter, CHUNK), bf16),
            pltpu.VMEM((CHUNKS, rows, CHUNK), bf16),
            pltpu.VMEM((CHUNKS, rows, CHUNK), bf16),
            pltpu.VMEM((rows, CHUNK), bf16),
            pltpu.VMEM((nz, 2, CHUNKS, q_rows, HEAD_SIZE), bf16),
            pltpu.VMEM((CHUNKS, nz, HEAD_SIZE, lanes), bf16),
            pltpu.VMEM((CHUNKS, nz, 8, lanes), f32),
            pltpu.VMEM((HALF, nz, HEAD_SIZE, lanes), bf16),
            pltpu.VMEM((HALF, nz, 8, lanes), f32),
            pltpu.VMEM((HALF, nz, HEAD_SIZE, lanes), bf16),
            pltpu.VMEM((HALF, nz, 8, lanes), f32),
            pltpu.VMEM((HALF, nz, HEAD_SIZE, lanes), bf16),
            pltpu.VMEM((HALF, nz, 8, lanes), f32),
            pltpu.VMEM((2, HALF, lanes, HEAD_SIZE), f32),
            pltpu.VMEM((2, HALF, 2, lanes, HEAD_SIZE), f32),
            dma((CHUNKS, 2)), dma((steps,)),
            dma((steps, nz, 2)), dma((steps, nz)),
            dma((steps, nz)), dma((steps, nz)),
            dma((steps, 2, nz)), dma((steps, 2, nz)),
            dma((CHUNKS,)), dma((CHUNKS,)),
            dma((nz, 2)), dma((nz,)), dma, dma,
            dma((HALF, 2)), dma((HALF, 2)),
            dma((HALF, nz - 1, 2)), dma((HALF, nz - 1, 2)),
            dma((HALF, 2)), dma((HALF, 2)), dma,
        ],
        compiler_params=pltpu.CompilerParams(
            collective_id=0, has_side_effects=True, vmem_limit_bytes=60 << 20),
        cost_estimate=pl.CostEstimate(
            flops=4 * rows * depth * width, bytes_accessed=16 << 20, transcendentals=0),
        name="serve",
    )(tokens, w_kv.reshape(4, quarter, width), requests, qown, decoded_keys.transpose(1, 0, 2), decoded_values.transpose(1, 0, 2))
    out = out.reshape(CHUNKS, GROUPED, STEPS, forks, HEAD_SIZE).transpose(3, 2, 0, 1, 4)
    return out.reshape(forks, STEPS, CHUNKS * GROUPED * HEAD_SIZE)


def local(tokens, w_kv, page_target, queries, decoded_keys, decoded_values):
    axes = tuple(lax.axis_size(a) for a in ("groups", "section", "tp"))
    if axes == (2, 2, 2) and w_kv.shape[1] == CHUNKS * CHUNK:
        return serve(tokens, w_kv, page_target, queries, decoded_keys, decoded_values)
    gathered = lax.all_gather(tokens, "tp", axis=1, tiled=True)
    kv_width = w_kv.shape[1]
    projected_rows = jnp.dot(
        gathered,
        lax.all_gather(w_kv, ("section", "ep"), axis=0, tiled=True),
        preferred_element_type=jnp.float32,
    )
    page_rows = gathered.shape[0] // PAGE
    page_data = projected_rows.astype(jnp.bfloat16).reshape(page_rows, PAGE * kv_width)
    targets = page_target[:, 0]
    dest_count = lax.axis_size(("section", "ep"))
    capacity = max(2, 2 * page_rows // dest_count)
    same_target = targets[:, None] == targets[None, :]
    earlier = jnp.arange(page_rows)[None, :] < jnp.arange(page_rows)[:, None]
    ranks = jnp.sum((same_target & earlier).astype(jnp.int32), axis=1)
    slot_index = targets * capacity + ranks
    placed = slot_index[None, :] == jnp.arange(dest_count * capacity, dtype=jnp.int32)[:, None]
    outgoing = jnp.dot(
        placed.astype(jnp.bfloat16), page_data, preferred_element_type=jnp.float32
    ).astype(jnp.bfloat16)
    filled = jnp.sum(placed.astype(jnp.int32), axis=1)
    arrived, live_slots = (
        lax.all_to_all(
            outgoing.reshape(dest_count, capacity, PAGE, kv_width),
            ("section", "ep"),
            split_axis=0,
            concat_axis=0,
            tiled=True,
        ),
        lax.all_to_all(
            filled.reshape(dest_count, capacity),
            ("section", "ep"),
            split_axis=0,
            concat_axis=0,
            tiled=True,
        ),
    )
    head_pairs = kv_width // (2 * HEAD_SIZE)
    arrived = arrived.reshape(-1, head_pairs, 2, HEAD_SIZE)
    prompt_keys = arrived[:, :, 0]
    prompt_values = arrived[:, :, 1]
    slot_live = jnp.repeat(live_slots.reshape(-1), PAGE) > 0
    forks = queries.shape[0]
    steps = queries.shape[1]
    grouped_heads = QUERY_HEADS // KEY_VALUE_HEADS
    query_head_list = queries.reshape(forks, steps, head_pairs, grouped_heads, HEAD_SIZE)
    latest_keys = decoded_keys.reshape(forks, steps, head_pairs, HEAD_SIZE)
    latest_values = decoded_values.reshape(forks, steps, head_pairs, HEAD_SIZE)
    inv_root = 1.0 / math.sqrt(HEAD_SIZE)
    prompt_scores = (
        jnp.einsum(
            "fsgjd,tgd->gfsjt", query_head_list, prompt_keys, preferred_element_type=jnp.float32
        )
        * inv_root
    )
    prompt_scores = jnp.where(slot_live, prompt_scores, -jnp.inf)
    fresh_scores = (
        jnp.einsum(
            "fsgjd,fugd->gfsju", query_head_list, latest_keys, preferred_element_type=jnp.float32
        )
        * inv_root
    )
    causal = jnp.arange(steps)[None, :] <= jnp.arange(steps)[:, None]
    fresh_scores = jnp.where(causal[None, None, :, None, :], fresh_scores, -jnp.inf)
    peak_score = jnp.maximum(jnp.max(prompt_scores, -1), jnp.max(fresh_scores, -1))[..., None]
    prompt_exp = jnp.exp(prompt_scores - peak_score)
    fresh_exp = jnp.exp(fresh_scores - peak_score)
    normalizer = jnp.sum(prompt_exp, -1, keepdims=True) + jnp.sum(fresh_exp, -1, keepdims=True)
    prompt_weights = (prompt_exp / normalizer).astype(jnp.bfloat16)
    fresh_weights = (fresh_exp / normalizer).astype(jnp.bfloat16)
    combined = jnp.einsum(
        "gfsjt,tgd->fsgjd", prompt_weights, prompt_values, preferred_element_type=jnp.float32
    )
    combined = combined + jnp.einsum(
        "gfsju,fugd->fsgjd", fresh_weights, latest_values, preferred_element_type=jnp.float32
    )
    return combined.reshape(forks, steps, -1).astype(jnp.bfloat16)


def solution(mesh):
    in_specs = (
        P(("groups", "section", "ep"), "tp"),
        P(("section", "ep"), "tp"),
        P(("groups", "section", "ep"), None),
        P(("groups", "section", "ep"), None, "tp"),
        P(("groups", "section", "ep"), None, "tp"),
        P(("groups", "section", "ep"), None, "tp"),
    )
    out_specs = P(("groups", "section", "ep"), None, "tp")
    return jax.shard_map(local, mesh=mesh, in_specs=in_specs, out_specs=out_specs, check_vma=False)
```
